512 devices in a mesh: row: 32 (over x, z_hi, y), col: 16 (over z_lo, core).
Axes of the slice: x: 4, y: 4, z: 16 (z_hi: 2, z_lo: 8; z = z_hi * 8 + z_lo), core: 2. Of those that a mesh axis runs over, the one named last changes fastest.
Arguments:
- positions: float32 [3, 262144], P(None, ('row', 'col')), may hold values from 0 to 2.4
- vel_half: float32 [3, 262144], P(None, ('row', 'col')), may hold values from -1.2 to 1.2
- charges: float32 [262144], P(('row', 'col')), may hold values from -1 to 1
- types: int32 [262144], P(('row', 'col')), may hold values from 0 to 17
- six_table: float32 [18, 18], replicated, may hold values from 0.05 to 0.25
- twelve_table: float32 [18, 18], replicated, may hold values from 0.0005 to 0.003
- tile_pairs: int32 [32, 16, 2, 128], P('row', 'col'), may hold values from 0 to 127, as said below
- pair_counts: int32 [32, 16], P('row', 'col'), may hold values from 16 to 128, as said below
Outputs:
- positions_new: float32 [3, 262144], P(None, ('row', 'col'))
- force_new: float32 [3, 262144], P(None, ('row', 'col'))
- velocity_new: float32 [3, 262144], P(None, ('row', 'col'))
The draws below stay inside these ranges and needn't reach their ends.
Inputs may be any that keep to these rules, and one draw needn't show every extreme that they name: `tile_pairs`: within one device's list all 128 slots are distinct tile pairs with indices in range of the two blocks; slots from pair_counts on hold valid pairs that are not used. Some device has a full list in every draw. `pair_counts`: each device's count is 128, 64, 32 or 16, and some device holds 128 in every draw.
All inputs are finite; a program needn't handle non-finite values.
Results may differ from the reference program's by a relative error of at most 0.0022.
Values sent between devices are 32-bit elements; how exact they have to be, the bound alone decides.
No kernel may reach another device: no remote copies, remote signals or barrier semaphores. Data moves between devices by JAX's collectives and lax.ppermute only.
A program may use at most 64 MiB of HBM per device.

```python
import math
import jax
import jax.numpy as jnp
from jax import lax

TILE_ATOMS = 128
TILES_DEV = 4
BEAD_TYPES = 18
PAIR_SLOTS = 128
ATOMS = 262144
N_ROW = 32
N_COL = 16


def draw_tile_pairs(key, part):
    key = jax.random.fold_in(key, 11)
    row_tiles = N_COL * TILES_DEV
    col_tiles = N_ROW * TILES_DEV
    device_keys = jax.random.split(key, N_ROW * N_COL)

    def one_device(device_key):
        order = jax.random.permutation(device_key, row_tiles * col_tiles)[:PAIR_SLOTS]
        return jnp.stack([order // col_tiles, order % col_tiles]).astype(jnp.int32)
    return jax.vmap(one_device)(device_keys).reshape(N_ROW, N_COL, 2, PAIR_SLOTS)


def draw_pair_counts(key, part):
    key = jax.random.fold_in(key, 23)
    shift_key, full_key = jax.random.split(key)
    shifts = jax.random.randint(shift_key, (N_ROW * N_COL,), 0, 4)
    counts = jnp.right_shift(jnp.full((N_ROW * N_COL,), PAIR_SLOTS, jnp.int32), shifts.astype(jnp.int32))
    chosen = jax.random.randint(full_key, (), 0, N_ROW * N_COL)
    counts = jnp.where(jnp.arange(N_ROW * N_COL) == chosen, PAIR_SLOTS, counts)
    return counts.reshape(N_ROW, N_COL).astype(jnp.int32)


def set_ends(entries, key, least, largest):
    longest = entries.shape.index(max(entries.shape))
    spots = []
    for shift in (0, 1):
        where = [jax.random.randint(jax.random.fold_in(key, axis), (), 0, length) for axis, length in enumerate(entries.shape)]
        where[longest] = (where[longest] + shift) % entries.shape[longest]
        spots.append(tuple(where))
    return entries.at[spots[0]].set(least).at[spots[1]].set(largest)


def level_of(stream_key, extent, pieces, least, top_value):
    factor_of = 1.0
    for axis_at, parts in pieces:
        heights = jax.random.uniform(jax.random.fold_in(jax.random.fold_in(stream_key, 6), axis_at), (parts,), jnp.float32, least / len(pieces), top_value / len(pieces))
        factor_of = factor_of * jnp.repeat(jnp.exp(heights), extent[axis_at] // parts).reshape((-1,) + (1,) * (len(extent) - 1 - axis_at))
    return factor_of


def scatter_about(own_key, shape, deviation, most, pieces=(), kind=jnp.bfloat16):
    entries = deviation * jax.random.normal(own_key, shape, jnp.float32)
    if pieces:
        entries = entries * level_of(own_key, shape, pieces, -0.22, 0.18)
    return jnp.clip(entries, -most, most).astype(kind)


def setup_inputs(seed: int = 0) -> dict:
    splits = jax.random.split(jax.random.key(seed), 9)
    return {
        "positions": jnp.clip(2.4 * jax.random.uniform(splits[0], (3, ATOMS), jnp.float32) ** level_of(splits[0], (3, ATOMS), ((1, 512),), -0.2, 0.2), 0.0, 2.4),
        "vel_half": scatter_about(splits[1], (3, ATOMS), 0.2, 1.2, ((1, 512),), jnp.float32),
        "charges": jnp.clip(jax.random.uniform(splits[2], (ATOMS,), jnp.float32, -1.0, 1.0) * level_of(splits[2], (ATOMS,), ((0, 512),), -0.4, 0.0), -1.0, 1.0),
        "types": set_ends(jax.random.randint(splits[3], (ATOMS,), 0, BEAD_TYPES), jax.random.fold_in(splits[3], 1), 0, BEAD_TYPES - 1).astype(jnp.int32),
        "six_table": jnp.clip(jnp.exp(jax.random.uniform(splits[4], (BEAD_TYPES, BEAD_TYPES), jnp.float32, math.log(0.05), math.log(0.25))), 0.05, 0.25),
        "twelve_table": jnp.clip(jnp.exp(jax.random.uniform(splits[5], (BEAD_TYPES, BEAD_TYPES), jnp.float32, math.log(0.0005), math.log(0.003))), 0.0005, 0.003),
        "tile_pairs": draw_tile_pairs(jax.random.fold_in(splits[8], 71), 0),
        "pair_counts": draw_pair_counts(jax.random.fold_in(splits[8], 71), 0),
    }


TIME_STEP = 0.02
HALF_KICK = 0.01 / 72.0
SOFT_CORE = 0.5
COULOMB = 9.262364
REACTION = 0.28935185
INV_CUT_SQ = 1.0 / 1.44

def pair_forces(pos_i, pos_j, charge_i, charge_j, six_coef, twelve_coef, keep_pair):
    offset = pos_i[:, :, :, None] - pos_j[:, :, None, :]
    dist_sq = offset[0] * offset[0] + offset[1] * offset[1] + offset[2] * offset[2]
    soft_sq = dist_sq + SOFT_CORE
    inverse = 1.0 / soft_sq
    inverse_sq = inverse * inverse
    inverse_four = inverse_sq * inverse_sq
    dispersion = 12.0 * twelve_coef * inverse_four * inverse_sq * inverse - 6.0 * six_coef * inverse_four
    coulomb = COULOMB * charge_i[:, :, None] * charge_j[:, None, :] * (inverse * lax.rsqrt(soft_sq) - 2.0 * REACTION)
    switch = jnp.maximum(1.0 - dist_sq * INV_CUT_SQ, 0.0)
    scalar = jnp.where(keep_pair, (dispersion + coulomb) * switch * switch, 0.0)
    product = scalar[None] * offset
    return (lax.optimization_barrier(jnp.sum(product, axis=3)), -lax.optimization_barrier(jnp.sum(product, axis=2)))

def reference(positions, vel_half, charges, types, six_table, twelve_table, tile_pairs, pair_counts):
    positions_new = positions + TIME_STEP * vel_half
    atoms_dev = TILES_DEV * TILE_ATOMS
    grid_pos = positions_new.reshape(3, N_ROW, N_COL, atoms_dev)
    grid_charge = charges.reshape(N_ROW, N_COL, atoms_dev)
    grid_types = types.reshape(N_ROW, N_COL, atoms_dev)
    upper_pair = lax.broadcasted_iota(jnp.int32, (TILE_ATOMS, TILE_ATOMS), 0) < lax.broadcasted_iota(jnp.int32, (TILE_ATOMS, TILE_ATOMS), 1)
    slot_ids = jnp.arange(PAIR_SLOTS, dtype=jnp.int32)

    def device_step(device, total):
        row_index = (device // N_COL).astype(jnp.int32)
        col_index = (device % N_COL).astype(jnp.int32)
        row_pos = lax.dynamic_index_in_dim(grid_pos, row_index, 1, keepdims=False).reshape(3, N_COL * TILES_DEV, TILE_ATOMS)
        col_pos = lax.dynamic_index_in_dim(grid_pos, col_index, 2, keepdims=False).reshape(3, N_ROW * TILES_DEV, TILE_ATOMS)
        row_charge = lax.dynamic_index_in_dim(grid_charge, row_index, 0, keepdims=False).reshape(N_COL * TILES_DEV, TILE_ATOMS)
        col_charge = lax.dynamic_index_in_dim(grid_charge, col_index, 1, keepdims=False).reshape(N_ROW * TILES_DEV, TILE_ATOMS)
        row_types = lax.dynamic_index_in_dim(grid_types, row_index, 0, keepdims=False).reshape(N_COL * TILES_DEV, TILE_ATOMS)
        col_types = lax.dynamic_index_in_dim(grid_types, col_index, 1, keepdims=False).reshape(N_ROW * TILES_DEV, TILE_ATOMS)
        row_list = lax.dynamic_index_in_dim(tile_pairs, row_index, 0, keepdims=False)
        slot_table = lax.dynamic_index_in_dim(row_list, col_index, 0, keepdims=False)
        live_count = lax.dynamic_index_in_dim(lax.dynamic_index_in_dim(pair_counts, row_index, 0, keepdims=False), col_index, 0, keepdims=False)
        first = slot_table[0]
        second = slot_table[1]
        is_live = slot_ids < live_count
        same_tile = (second // TILES_DEV == row_index) & (first == col_index * TILES_DEV + second % TILES_DEV)
        keep_pair = is_live[:, None, None] & (jnp.logical_not(same_tile)[:, None, None] | upper_pair[None])
        type_i = row_types[first]
        type_j = col_types[second]
        six_coef = six_table[type_i[:, :, None], type_j[:, None, :]]
        twelve_coef = twelve_table[type_i[:, :, None], type_j[:, None, :]]
        force_i, force_j = pair_forces(row_pos[:, first], col_pos[:, second], row_charge[first], col_charge[second], six_coef, twelve_coef, keep_pair)
        row_force = jnp.zeros((3, N_COL * TILES_DEV, TILE_ATOMS), jnp.float32).at[:, first].add(force_i)
        col_force = jnp.zeros((3, N_ROW * TILES_DEV, TILE_ATOMS), jnp.float32).at[:, second].add(force_j)
        total = total.at[:, row_index].add(row_force.reshape(3, N_COL, atoms_dev))
        total = total.at[:, :, col_index].add(col_force.reshape(3, N_ROW, atoms_dev))
        return total
    total = jnp.zeros((3, N_ROW, N_COL, atoms_dev), jnp.float32)
    total = lax.fori_loop(0, N_ROW * N_COL, device_step, total)
    force_new = total.reshape(3, N_ROW * N_COL * atoms_dev)
    velocity_new = vel_half + HALF_KICK * force_new
    return (positions_new, force_new, velocity_new)
```

```python
import functools
import jax
import jax.numpy as jnp
from jax import lax
from jax.experimental import pallas as pl
from jax.experimental.pallas import tpu as pltpu
from jax.sharding import PartitionSpec as P

TILE_ATOMS = 128
BEAD_TYPES = 18
LANES = 128

TIME_STEP = 0.02
HALF_KICK = 0.01 / 72.0
SOFT_CORE = 0.5
COULOMB = 9.262364
REACTION = 0.28935185
CUT_SQ = 1.44
CENTRE = 1.2

X_SIZE = 4
ZH_SIZE = 2
Y_SIZE = 4
TYPE_ROWS = 24
UNROLL = 2


def split_three(values):
    upper = values.astype(jnp.bfloat16).astype(jnp.float32)
    rest = values - upper
    middle = rest.astype(jnp.bfloat16).astype(jnp.float32)
    return upper, middle, rest - middle


def pair_kernel(
    pairs_ref, count_ref, row_ref, col_ref, table_ref, row_force, col_force, lhs_ref
):
    row_tiles = row_ref.shape[0]
    tiles_dev = 4
    my_row = lax.axis_index("row")
    my_col = lax.axis_index("col")
    my_zh = (my_row // Y_SIZE) % ZH_SIZE
    f32 = jnp.float32
    sub8 = lax.broadcasted_iota(jnp.int32, (8, LANES), 0)
    type_rows = lax.broadcasted_iota(jnp.int32, (TYPE_ROWS, LANES), 0).astype(f32)
    lane = lax.broadcasted_iota(jnp.int32, (TILE_ATOMS, LANES), 1)
    is_charge = (lane % 8 == 5) & (lane < 32)
    is_dist = (lane % 8 != 5) & (lane < 32)
    is_six = (lane >= 32) & (lane < 80)
    is_twelve = lane >= 80
    scale = jnp.where(sub8 < 3, -2.0, jnp.where(sub8 == 5, COULOMB / CUT_SQ**2, 0.0)).astype(f32)

    row_force[...] = jnp.zeros(row_force.shape, f32)
    col_force[...] = jnp.zeros(col_force.shape, f32)

    def prepare(tile, carry):
        block = row_ref[tile]
        left = block * scale
        left = jnp.where(sub8 == 3, 1.0, left)
        left = jnp.where(sub8 == 4, block[3:4] + SOFT_CORE, left)
        upper, middle, _ = split_three(left)
        hot = (jnp.broadcast_to(block[6:7], (TYPE_ROWS, LANES)) == type_rows).astype(f32)
        coefs = jnp.dot(
            table_ref[...], hot.astype(jnp.bfloat16), preferred_element_type=f32
        )
        whole = jnp.concatenate([upper, upper, middle, middle, coefs], axis=0).T
        for part, keep in enumerate((is_dist, is_charge, is_six, is_twelve)):
            lhs_ref[tile, part * TILE_ATOMS : (part + 1) * TILE_ATOMS, :] = jnp.where(
                keep, whole, 0.0
            ).astype(jnp.bfloat16)
        return carry

    lax.fori_loop(0, row_tiles, prepare, 0)

    def one_pair(first, place, same):
        right = col_ref[place]
        left = row_ref[first]
        upper, middle, lower = split_three(right)
        hot = (jnp.broadcast_to(right[6:7], (TYPE_ROWS, LANES)) == type_rows).astype(f32)
        rhs = jnp.concatenate(
            [upper, middle, upper, middle, hot, hot, hot, hot], axis=0
        ).astype(jnp.bfloat16)
        looked = jnp.dot(lhs_ref[first], rhs, preferred_element_type=f32)
        soft_sq = looked[0:128]
        charge = looked[128:256]
        six = looked[256:384]
        twelve = looked[384:512]
        root = lax.rsqrt(soft_sq)
        inverse = root * root
        inverse_two = inverse * inverse
        inverse_four = inverse_two * inverse_two
        dispersion = inverse_four * (twelve * (inverse_two * inverse) - six)
        coulomb = charge * (inverse * root - 2.0 * REACTION)
        switch = jnp.maximum((CUT_SQ + SOFT_CORE) - soft_sq, 0.0)
        scalar = (dispersion + coulomb) * (switch * switch)
        if same is not None:
            at_i = lax.broadcasted_iota(jnp.int32, (TILE_ATOMS, LANES), 0)
            scalar = jnp.where((at_i < lane) | jnp.logical_not(same), scalar, 0.0)
        high = scalar.astype(jnp.bfloat16)
        low = (scalar - high.astype(f32)).astype(jnp.bfloat16)
        right_x = jnp.concatenate([upper, middle, lower, lower], axis=0).astype(jnp.bfloat16)
        left_x = jnp.concatenate([*split_three(left), jnp.zeros_like(left)], axis=0).astype(
            jnp.bfloat16
        )
        nt = (((1,), (1,)), ((), ()))
        nn = (((1,), (0,)), ((), ()))
        sums_i = lax.dot_general(right_x, high, nt, preferred_element_type=f32)
        sums_i += lax.dot_general(right_x, low, nt, preferred_element_type=f32)
        sums_j = lax.dot_general(left_x, high, nn, preferred_element_type=f32)
        sums_j += lax.dot_general(left_x, low, nn, preferred_element_type=f32)
        sums_i = sums_i[0:8] + sums_i[8:16] + sums_i[16:24]
        sums_j = sums_j[0:8] + sums_j[8:16] + sums_j[16:24]
        force_i = left * sums_i[4:5] - sums_i
        force_j = right * sums_j[4:5] - sums_j
        row_force[first] += force_i[0:4]
        col_force[place] += force_j[0:4]

    def step(index, carry):
        found = []
        for part in range(UNROLL):
            slot = index * UNROLL + part
            first = pairs_ref[0, 0, 0, slot]
            second = pairs_ref[0, 0, 1, slot]
            owner = second // tiles_dev
            same = (owner == my_row) & (first == my_col * tiles_dev + second % tiles_dev)
            far = ((owner // Y_SIZE) % ZH_SIZE + my_zh) % ZH_SIZE
            place = (
                ((owner // (Y_SIZE * ZH_SIZE)) * Y_SIZE + owner % Y_SIZE) * ZH_SIZE + far
            ) * tiles_dev + second % tiles_dev
            found.append((first, place, same))
        any_same = functools.reduce(jnp.logical_or, [same for _, _, same in found])

        @pl.when(any_same)
        def _():
            for first, place, same in found:
                one_pair(first, place, same)

        @pl.when(jnp.logical_not(any_same))
        def _():
            for first, place, _ in found:
                one_pair(first, place, None)

        return carry

    lax.fori_loop(0, count_ref[0, 0] // UNROLL, step, 0)


def shards(positions, vel_half, charges, types, six_table, twelve_table, tile_pairs, pair_counts):
    atoms_dev = positions.shape[1]
    tiles_dev = atoms_dev // TILE_ATOMS
    n_row = X_SIZE * ZH_SIZE * Y_SIZE
    n_col = lax.axis_size("col")
    n_xy = X_SIZE * Y_SIZE
    xy_groups = [
        [(x * ZH_SIZE + zh) * Y_SIZE + y for x in range(X_SIZE) for y in range(Y_SIZE)]
        for zh in range(ZH_SIZE)
    ]
    zh_swap = [
        ((x * ZH_SIZE + zh) * Y_SIZE + y, (x * ZH_SIZE + 1 - zh) * Y_SIZE + y)
        for x in range(X_SIZE)
        for zh in range(ZH_SIZE)
        for y in range(Y_SIZE)
    ]

    moved_pos = positions + TIME_STEP * vel_half
    centred = (moved_pos - CENTRE).reshape(3, tiles_dev, TILE_ATOMS)
    square = centred[0] * centred[0] + centred[1] * centred[1] + centred[2] * centred[2]
    block = jnp.stack(
        [
            centred[0],
            centred[1],
            centred[2],
            square,
            jnp.ones_like(square),
            charges.reshape(tiles_dev, TILE_ATOMS),
            types.astype(jnp.float32).reshape(tiles_dev, TILE_ATOMS),
            jnp.zeros_like(square),
        ],
        axis=1,
    )
    pad = ((0, TYPE_ROWS - BEAD_TYPES), (0, TYPE_ROWS - BEAD_TYPES))
    six = jnp.pad(six_table.T * (6.0 / CUT_SQ**2), pad)
    twelve = jnp.pad(twelve_table.T * (12.0 / CUT_SQ**2), pad)
    parts = []
    for table in (six, twelve):
        upper = lax.reduce_precision(table, 8, 7)
        parts += [upper, table - upper]
    tables = jnp.concatenate(parts, axis=0).astype(jnp.bfloat16)

    rows_dev = tiles_dev * 8
    block = block.reshape(rows_dev, LANES)
    far_block = lax.ppermute(block, "row", zh_swap)
    row_blocks = lax.all_to_all(
        jnp.broadcast_to(block[None], (n_col, rows_dev, LANES)), "col", 0, 0
    )
    both = jnp.concatenate([block, far_block], axis=0)
    col_blocks = lax.all_to_all(
        jnp.broadcast_to(both[None], (n_xy, 2 * rows_dev, LANES)),
        "row",
        0,
        0,
        axis_index_groups=xy_groups,
    )
    row_tiles = n_col * tiles_dev
    col_tiles = n_row * tiles_dev
    smem = pl.BlockSpec(memory_space=pltpu.SMEM)
    vmem = pl.BlockSpec(memory_space=pltpu.VMEM)
    row_force, col_force = pl.pallas_call(
        pair_kernel,
        out_shape=(
            jax.ShapeDtypeStruct((row_tiles, 4, LANES), jnp.float32),
            jax.ShapeDtypeStruct((col_tiles, 4, LANES), jnp.float32),
        ),
        in_specs=[smem, smem, vmem, vmem, vmem],
        out_specs=(vmem, vmem),
        scratch_shapes=[pltpu.VMEM((row_tiles, 4 * TILE_ATOMS, LANES), jnp.bfloat16)],
        compiler_params=pltpu.CompilerParams(vmem_limit_bytes=32 * 2**20),
        name="pair_forces",
    )(
        tile_pairs,
        pair_counts,
        row_blocks.reshape(row_tiles, 8, LANES),
        col_blocks.reshape(col_tiles, 8, LANES),
        tables,
    )
    col_parts = lax.all_to_all(
        col_force.reshape(n_xy, ZH_SIZE * tiles_dev * 4, LANES),
        "row",
        0,
        0,
        axis_index_groups=xy_groups,
    )
    col_sum = jnp.sum(col_parts, axis=0)
    half = tiles_dev * 4
    far_sum = lax.ppermute(col_sum[half:], "row", zh_swap)
    row_parts = lax.all_to_all(
        row_force.reshape(n_col, tiles_dev * 4, LANES), "col", 0, 0
    )
    force = jnp.sum(row_parts, axis=0) + col_sum[:half] + far_sum
    force_new = force.reshape(tiles_dev, 4, TILE_ATOMS)[:, 0:3].transpose(1, 0, 2)
    force_new = force_new.reshape(3, atoms_dev)
    velocity_new = vel_half + HALF_KICK * force_new
    return (moved_pos, force_new, velocity_new)


def solution(mesh):
    placed = (
        P(None, ("row", "col")),
        P(None, ("row", "col")),
        P(("row", "col")),
        P(("row", "col")),
        P(),
        P(),
        P("row", "col", None, None),
        P("row", "col"),
    )
    return jax.shard_map(
        shards,
        mesh=mesh,
        in_specs=placed,
        out_specs=(P(None, ("row", "col")), P(None, ("row", "col")), P(None, ("row", "col"))),
        check_vma=False,
    )
```

```python
import functools
import jax
import jax.numpy as jnp
from jax import lax
from jax.experimental import pallas as pl
from jax.experimental.pallas import tpu as pltpu
from jax.sharding import PartitionSpec as P

TILE_ATOMS = 128
TILES_DEV = 4
BEAD_TYPES = 18
LANES = 128

TIME_STEP = 0.02
HALF_KICK = 0.01 / 72.0
SOFT_CORE = 0.5
COULOMB = 9.262364
REACTION = 0.28935185
CUT_SQ = 1.44
CENTRE = 1.2

X_SIZE = 4
ZH_SIZE = 2
Y_SIZE = 4
N_COL = 16
CORES = 2
CHANNELS = 6
TYPE_ROWS = 24
UNROLL = 16
PREPARED = 4

def split_three(values):
    upper = values.astype(jnp.bfloat16).astype(jnp.float32)
    rest = values - upper
    middle = rest.astype(jnp.bfloat16).astype(jnp.float32)
    return upper, middle, rest - middle


def pair_kernel(
    pairs_ref, count_ref, own_ref, other_ref, col_ref, table_ref,
    own_force, other_force, col_force,
    row_block, col_block, row_sum, col_sum, lhs_ref, scalar_ref
):
    tiles_dev = TILES_DEV
    my_row = lax.axis_index("row")
    my_col = lax.axis_index("col")
    my_zh = (my_row // Y_SIZE) % ZH_SIZE
    my_core = my_col % CORES
    half_tiles = row_block.shape[0] // CORES
    f32 = jnp.float32
    bf16 = jnp.bfloat16
    sub8 = lax.broadcasted_iota(jnp.int32, (8, LANES), 0)
    type_rows = lax.broadcasted_iota(jnp.int32, (TYPE_ROWS, LANES), 0).astype(f32)
    lane = lax.broadcasted_iota(jnp.int32, (TILE_ATOMS, LANES), 1)
    is_charge = (lane % 8 == 4) & (lane < 32)
    is_dist = (lane % 8 != 4) & (lane < 32)
    is_six = (lane >= 32) & (lane < 80)
    is_twelve = lane >= 80
    scale = jnp.where(sub8 < 3, -2.0, jnp.where(sub8 == 4, COULOMB / CUT_SQ**2, 0.0)).astype(f32)
    one_zero = jnp.where(lax.broadcasted_iota(jnp.int32, (2, LANES), 0) == 0, 1.0, 0.0).astype(f32)

    row_sum[...] = jnp.zeros(row_sum.shape, f32)
    col_sum[...] = jnp.zeros(col_sum.shape, f32)
    scalar_ref[...] = jnp.zeros(scalar_ref.shape, bf16)

    def hot_types(block):
        return (jnp.broadcast_to(block[5:6], (TYPE_ROWS, LANES)) == type_rows).astype(f32)

    def spread(source, owner, target, start):
        rows = source[owner]
        for tile in range(tiles_dev):
            piece = rows[CHANNELS * tile : CHANNELS * (tile + 1)]
            target[start + owner * tiles_dev + tile] = jnp.concatenate([piece, one_zero], axis=0)

    def spread_owners(index, carry):
        spread(own_ref, index, row_block, 0)
        spread(other_ref, index, row_block, half_tiles)
        for part in range(4):
            spread(col_ref, index * 4 + part, col_block, 0)
        return carry

    lax.fori_loop(0, own_ref.shape[0], spread_owners, 0)

    def prepare(index, carry):
        wholes = []
        for part in range(PREPARED):
            block = row_block[index * PREPARED + part]
            left = block * scale
            left = jnp.where(sub8 == 3, 1.0, left)
            left = jnp.where(sub8 == 6, block[3:4] + SOFT_CORE, left)
            upper, middle, _ = split_three(left)
            coefs = jnp.dot(
                table_ref[...], hot_types(block).astype(bf16), preferred_element_type=f32
            )
            wholes.append(jnp.concatenate([upper, upper, middle, middle, coefs], axis=0))
        for part in range(PREPARED):
            whole = wholes[part].T
            for which, keep in enumerate((is_dist, is_charge, is_six, is_twelve)):
                lhs_ref[
                    index * PREPARED + part, which * TILE_ATOMS : (which + 1) * TILE_ATOMS, :
                ] = jnp.where(keep, whole, 0.0).astype(bf16)
        return carry

    lax.fori_loop(0, row_block.shape[0] // PREPARED, prepare, 0)

    def features(first, place):
        right = col_block[place]
        upper, middle, _ = split_three(right)
        hot = hot_types(right)
        rhs = jnp.concatenate([upper, middle, upper, middle, hot, hot, hot, hot], axis=0)
        return jnp.dot(lhs_ref[first], rhs.astype(bf16), preferred_element_type=f32)

    def scalars(looked, same, part):
        soft_sq = looked[0:128]
        charge = looked[128:256]
        six = looked[256:384]
        twelve = looked[384:512]
        root = lax.rsqrt(soft_sq)
        inverse = root * root
        inverse_two = inverse * inverse
        inverse_four = inverse_two * inverse_two
        dispersion = inverse_four * (twelve * (inverse_two * inverse) - six)
        coulomb = charge * (inverse * root - 2.0 * REACTION)
        switch = jnp.maximum((CUT_SQ + SOFT_CORE) - soft_sq, 0.0)
        scalar = (dispersion + coulomb) * (switch * switch)
        if same is not None:
            at_i = lax.broadcasted_iota(jnp.int32, (TILE_ATOMS, LANES), 0)
            scalar = jnp.where((at_i < lane) | jnp.logical_not(same), scalar, 0.0)
        high = scalar.astype(bf16)
        scalar_ref[part, 0] = high
        scalar_ref[part, 1] = (scalar - high.astype(f32)).astype(bf16)

    def add_forces(first, place, part):
        left = row_block[first]
        right = col_block[place]
        left_x = jnp.concatenate([*split_three(left), jnp.zeros_like(left)], axis=0).astype(bf16)
        right_x = jnp.concatenate([*split_three(right), jnp.zeros_like(right)], axis=0).astype(bf16)
        high = scalar_ref[part, 0]
        low = scalar_ref[part, 1]
        sums_i = lax.dot_general(
            jnp.concatenate([right_x, right_x], axis=1),
            jnp.concatenate([high, low], axis=1),
            (((1,), (1,)), ((), ())),
            preferred_element_type=f32,
        )
        sums_j = jnp.dot(
            jnp.concatenate([left_x, left_x], axis=1),
            jnp.concatenate([high, low], axis=0),
            preferred_element_type=f32,
        )
        sums_i = sums_i[0:8] + sums_i[8:16] + sums_i[16:24]
        sums_j = sums_j[0:8] + sums_j[8:16] + sums_j[16:24]
        row_sum[first] += left * sums_i[6:7] - sums_i
        col_sum[place] += right * sums_j[6:7] - sums_j

    def find(slot):
        first = pairs_ref[0, 0, 0, slot]
        second = pairs_ref[0, 0, 1, slot]
        owner = second >> 2
        tile = second & 3
        same = (owner == my_row) & (first == my_col * tiles_dev + tile)
        far = ((owner >> 2) & 1) ^ my_zh
        place = ((owner & 24) << 2) | ((owner & 3) << 3) | (far << 2) | tile
        owner = first >> 2
        first = (((owner & 1) ^ my_core) << 5) | ((owner >> 1) << 2) | (first & 3)
        return first, place, same

    def step(index, before):
        found = [find(index * UNROLL + part) for part in range(UNROLL)]
        any_same = functools.reduce(jnp.logical_or, [same for _, _, same in found])

        def work(masked):
            looked = []
            for part, (first, place, _) in enumerate(found):
                looked.append(features(first, place))
                add_forces(before[2 * part], before[2 * part + 1], part)
            for part, (_, _, same) in enumerate(found):
                scalars(looked[part], same if masked else None, part)

        @pl.when(any_same)
        def _():
            work(True)

        @pl.when(jnp.logical_not(any_same))
        def _():
            work(False)

        return tuple(place for first, second, _ in found for place in (first, second))

    last = lax.fori_loop(
        0, count_ref[0, 0] // UNROLL, step, tuple(jnp.int32(0) for _ in range(2 * UNROLL))
    )
    for part in range(UNROLL):
        add_forces(last[2 * part], last[2 * part + 1], part)
    own_force[...] = row_sum[0:half_tiles, 0:4, :]
    other_force[...] = row_sum[half_tiles:, 0:4, :]
    col_force[...] = col_sum[:, 0:4, :]


def shards(positions, vel_half, charges, types, six_table, twelve_table, tile_pairs, pair_counts):
    atoms_dev = positions.shape[1]
    tiles_dev = TILES_DEV
    n_row = X_SIZE * ZH_SIZE * Y_SIZE
    n_col = N_COL
    n_xy = X_SIZE * Y_SIZE
    n_zl = n_col // CORES
    n_z = ZH_SIZE * n_zl
    my_zh = (lax.axis_index("row") // Y_SIZE) % ZH_SIZE
    my_zl = lax.axis_index("col") // CORES
    xy_groups = [
        [(x * ZH_SIZE + zh) * Y_SIZE + y for x in range(X_SIZE) for y in range(Y_SIZE)]
        for zh in range(ZH_SIZE)
    ]
    z_groups = [
        [
            ((x * ZH_SIZE + zh) * Y_SIZE + y) * n_col + zl * CORES + core
            for zh in range(ZH_SIZE)
            for zl in range(n_zl)
        ]
        for x in range(X_SIZE)
        for y in range(Y_SIZE)
        for core in range(CORES)
    ]
    zl_groups = [list(range(core, n_col, CORES)) for core in range(CORES)]
    core_swap = [(at, at ^ 1) for at in range(n_col)]
    zh_swap = [(at, at ^ Y_SIZE) for at in range(n_row)]

    moved_pos = positions + TIME_STEP * vel_half
    centred = (moved_pos - CENTRE).reshape(3, tiles_dev, TILE_ATOMS)
    square = centred[0] * centred[0] + centred[1] * centred[1] + centred[2] * centred[2]
    block = jnp.stack(
        [
            centred[0],
            centred[1],
            centred[2],
            square,
            charges.reshape(tiles_dev, TILE_ATOMS),
            types.astype(jnp.float32).reshape(tiles_dev, TILE_ATOMS),
        ],
        axis=1,
    )
    pad = ((0, TYPE_ROWS - BEAD_TYPES), (0, TYPE_ROWS - BEAD_TYPES))
    six = jnp.pad(six_table.T * (6.0 / CUT_SQ**2), pad)
    twelve = jnp.pad(twelve_table.T * (12.0 / CUT_SQ**2), pad)
    parts = []
    for table in (six, twelve):
        upper = lax.reduce_precision(table, 8, 7)
        parts += [upper, table - upper]
    tables = jnp.concatenate(parts, axis=0).astype(jnp.bfloat16)

    rows_dev = tiles_dev * CHANNELS
    block = block.reshape(rows_dev, LANES)
    far_block = lax.ppermute(block, "row", zh_swap)
    own_blocks = lax.all_to_all(
        jnp.broadcast_to(block[None], (n_zl, rows_dev, LANES)),
        "col",
        0,
        0,
        axis_index_groups=zl_groups,
    )
    far_block, own_blocks = lax.optimization_barrier((far_block, own_blocks))
    other_blocks = lax.ppermute(own_blocks, "col", core_swap)
    both = jnp.stack([block, far_block], axis=0)
    col_blocks = lax.all_to_all(
        jnp.broadcast_to(both[None], (n_xy, ZH_SIZE, rows_dev, LANES)),
        "row",
        0,
        0,
        axis_index_groups=xy_groups,
    )
    row_tiles = n_col * tiles_dev
    col_tiles = n_row * tiles_dev
    smem = pl.BlockSpec(memory_space=pltpu.SMEM)
    vmem = pl.BlockSpec(memory_space=pltpu.VMEM)
    own_force, other_force, col_force = pl.pallas_call(
        pair_kernel,
        out_shape=(
            jax.ShapeDtypeStruct((row_tiles // CORES, 4, LANES), jnp.float32),
            jax.ShapeDtypeStruct((row_tiles // CORES, 4, LANES), jnp.float32),
            jax.ShapeDtypeStruct((col_tiles, 4, LANES), jnp.float32),
        ),
        in_specs=[smem, smem, vmem, vmem, vmem, vmem],
        out_specs=(vmem, vmem, vmem),
        scratch_shapes=[
            pltpu.VMEM((row_tiles, 8, LANES), jnp.float32),
            pltpu.VMEM((col_tiles, 8, LANES), jnp.float32),
            pltpu.VMEM((row_tiles, 8, LANES), jnp.float32),
            pltpu.VMEM((col_tiles, 8, LANES), jnp.float32),
            pltpu.VMEM((row_tiles, 4 * TILE_ATOMS, LANES), jnp.bfloat16),
            pltpu.VMEM((UNROLL, 2, TILE_ATOMS, LANES), jnp.bfloat16),
        ],
        compiler_params=pltpu.CompilerParams(vmem_limit_bytes=32 * 2**20),
        name="pair_forces",
    )(
        tile_pairs,
        pair_counts,
        own_blocks,
        other_blocks,
        col_blocks.reshape(n_row, rows_dev, LANES),
        tables,
    )
    core_force = lax.ppermute(other_force, "col", core_swap)
    col_parts = lax.all_to_all(
        col_force.reshape(n_xy, ZH_SIZE * tiles_dev * 4, LANES),
        "row",
        0,
        0,
        axis_index_groups=xy_groups,
    )
    col_sum = jnp.sum(col_parts, axis=0)
    half = tiles_dev * 4
    row_sum = (own_force + core_force).reshape(1, n_zl, half, LANES)
    to_zh = lax.broadcasted_iota(jnp.int32, (ZH_SIZE, n_zl, half, LANES), 0)
    to_zl = lax.broadcasted_iota(jnp.int32, (ZH_SIZE, n_zl, half, LANES), 1)
    far_sum = jnp.where(to_zl == my_zl, col_sum[half:][None, None], 0.0)
    z_parts = lax.all_to_all(
        jnp.where(to_zh == my_zh, row_sum, far_sum).reshape(n_z, half, LANES),
        ("row", "col"),
        0,
        0,
        axis_index_groups=z_groups,
    )
    force = jnp.sum(z_parts, axis=0) + col_sum[:half]
    force_new = force.reshape(tiles_dev, 4, TILE_ATOMS)[:, 0:3].transpose(1, 0, 2)
    force_new = force_new.reshape(3, atoms_dev)
    velocity_new = vel_half + HALF_KICK * force_new
    return (moved_pos, force_new, velocity_new)


def solution(mesh):
    placed = (
        P(None, ("row", "col")),
        P(None, ("row", "col")),
        P(("row", "col")),
        P(("row", "col")),
        P(),
        P(),
        P("row", "col", None, None),
        P("row", "col"),
    )
    return jax.shard_map(
        shards,
        mesh=mesh,
        in_specs=placed,
        out_specs=(P(None, ("row", "col")), P(None, ("row", "col")), P(None, ("row", "col"))),
        check_vma=False,
    )
```

```python
import functools
import jax
import jax.numpy as jnp
from jax import lax
from jax.experimental import pallas as pl
from jax.experimental.pallas import tpu as pltpu
from jax.sharding import PartitionSpec as P

TILE_ATOMS = 128
TILES_DEV = 4
BEAD_TYPES = 18
LANES = 128

TIME_STEP = 0.02
HALF_KICK = 0.01 / 72.0
SOFT_CORE = 0.5
COULOMB = 9.262364
REACTION = 0.28935185
CUT_SQ = 1.44
CENTRE = 1.2

X_SIZE = 4
ZH_SIZE = 2
Y_SIZE = 4
N_COL = 16
CORES = 2
CHANNELS = 5
TYPE_ROWS = 24
UNROLL = 16
PREPARED = 16

def split_three(values):
    upper = values.astype(jnp.bfloat16).astype(jnp.float32)
    rest = values - upper
    middle = rest.astype(jnp.bfloat16).astype(jnp.float32)
    return upper, middle, rest - middle


def pack_kernel(positions_ref, vel_ref, charge_ref, type_ref, moved_ref, block_ref, blocks_ref):
    moved = positions_ref[...] + TIME_STEP * vel_ref[...]
    moved_ref[...] = moved
    centred = moved - CENTRE
    channels = [
        jnp.concatenate(
            [
                centred[axis : axis + 1, tile * TILE_ATOMS : (tile + 1) * TILE_ATOMS]
                for tile in range(TILES_DEV)
            ],
            axis=0,
        )
        for axis in range(3)
    ]
    channels += [charge_ref[...], type_ref[...].astype(jnp.float32)]
    for channel, values in enumerate(channels):
        block_ref[channel] = values
        for copy in range(blocks_ref.shape[0]):
            blocks_ref[copy, channel] = values


def hot_types(block):
    type_rows = lax.broadcasted_iota(jnp.int32, (TYPE_ROWS, LANES), 0).astype(jnp.float32)
    return (jnp.broadcast_to(block[5:6], (TYPE_ROWS, LANES)) == type_rows).astype(jnp.float32)


def spread(source, owner, target, start):
    x, y, z, charge, kind = [source[owner, channel] for channel in range(CHANNELS)]
    one = jnp.ones_like(x)
    channels = (x, y, z, x * x + y * y + z * z, charge, kind, one, jnp.zeros_like(x))
    for channel, values in enumerate(channels):
        target[pl.ds(start, TILES_DEV), channel, :] = values


def row_kernel(own_ref, other_ref, table_ref, row_block, lhs_ref):
    f32 = jnp.float32
    half_tiles = row_block.shape[0] // CORES
    sub8 = lax.broadcasted_iota(jnp.int32, (8, LANES), 0)
    scale = jnp.where(sub8 < 3, -2.0, jnp.where(sub8 == 4, COULOMB / CUT_SQ**2, 0.0)).astype(f32)

    n_zl = own_ref.shape[0] // ZH_SIZE
    start = ((lax.axis_index("row") // Y_SIZE) % ZH_SIZE) * n_zl

    def spread_owners(index, carry):
        spread(own_ref, start + index, row_block, index * TILES_DEV)
        spread(other_ref, start + index, row_block, half_tiles + index * TILES_DEV)
        return carry

    lax.fori_loop(0, n_zl, spread_owners, 0)

    def prepare(index, carry):
        wholes = []
        for part in range(PREPARED):
            block = row_block[index * PREPARED + part]
            left = block * scale
            left = jnp.where(sub8 == 3, 1.0, left)
            left = jnp.where(sub8 == 6, block[3:4] + SOFT_CORE, left)
            upper, middle, _ = split_three(left)
            coefs = jnp.dot(
                table_ref[...],
                hot_types(block).astype(jnp.bfloat16),
                preferred_element_type=f32,
            )
            wholes.append(jnp.concatenate([upper, upper, middle, middle, coefs], axis=0))
        for part in range(PREPARED):
            lhs_ref[index * PREPARED + part] = wholes[part].T.astype(jnp.bfloat16)
        return carry

    lax.fori_loop(0, row_block.shape[0] // PREPARED, prepare, 0)


def pair_kernel(
    pairs_ref, count_ref, row_block, lhs_ref, col_ref,
    own_force, other_force, col_force,
    col_block, row_sum, col_sum, scalar_ref
):
    tiles_dev = TILES_DEV
    my_row = lax.axis_index("row")
    my_col = lax.axis_index("col")
    my_zh = (my_row // Y_SIZE) % ZH_SIZE
    my_core = my_col % CORES
    half_tiles = row_block.shape[0] // CORES
    f32 = jnp.float32
    bf16 = jnp.bfloat16
    sub8 = lax.broadcasted_iota(jnp.int32, (8, LANES), 0)
    sub8 = lax.broadcasted_iota(jnp.int32, (8, LANES), 0)
    lane = lax.broadcasted_iota(jnp.int32, (TILE_ATOMS, LANES), 1)

    row_sum[...] = jnp.zeros(row_sum.shape, f32)
    col_sum[...] = jnp.zeros(col_sum.shape, f32)
    scalar_ref[...] = jnp.zeros(scalar_ref.shape, bf16)

    def spread_owners(index, carry):
        for part in range(4):
            owner = index * 4 + part
            spread(col_ref, owner, col_block, owner * TILES_DEV)
        return carry

    lax.fori_loop(0, col_ref.shape[0] // 4, spread_owners, 0)

    def features(first, place):
        right = col_block[place]
        upper, middle, _ = split_three(right)
        hot = hot_types(right)
        zero = jnp.zeros_like(hot)
        dist = [jnp.where(sub8 == 4, 0.0, part) for part in (upper, middle)]
        charge = [jnp.where(sub8 == 4, part, 0.0) for part in (upper, middle)]
        none = jnp.zeros((32, LANES), f32)
        rhs = [
            jnp.concatenate([*dist, *dist, zero, zero, zero, zero], axis=0),
            jnp.concatenate([*charge, *charge, zero, zero, zero, zero], axis=0),
            jnp.concatenate([none, hot, hot, zero, zero], axis=0),
            jnp.concatenate([none, zero, zero, hot, hot], axis=0),
        ]
        left = lhs_ref[first]
        looked = []
        for which in (0, 2):
            both = jnp.concatenate(rhs[which : which + 2], axis=1).astype(bf16)
            product = jnp.dot(left, both, preferred_element_type=f32)
            looked += [product[:, 0:LANES], product[:, LANES:]]
        return looked

    def scalars(looked, same, part):
        soft_sq, charge, six, twelve = looked
        root = lax.rsqrt(soft_sq)
        inverse = root * root
        inverse_two = inverse * inverse
        inverse_four = inverse_two * inverse_two
        dispersion = inverse_four * (twelve * (inverse_two * inverse) - six)
        coulomb = charge * (inverse * root - 2.0 * REACTION)
        switch = jnp.maximum((CUT_SQ + SOFT_CORE) - soft_sq, 0.0)
        scalar = (dispersion + coulomb) * (switch * switch)
        if same is not None:
            at_i = lax.broadcasted_iota(jnp.int32, (TILE_ATOMS, LANES), 0)
            scalar = jnp.where((at_i < lane) | jnp.logical_not(same), scalar, 0.0)
        high = scalar.astype(bf16)
        scalar_ref[part, 0] = high
        scalar_ref[part, 1] = (scalar - high.astype(f32)).astype(bf16)

    def add_forces(first, place, part):
        left = row_block[first]
        right = col_block[place]
        left_x = jnp.concatenate([*split_three(left), jnp.zeros_like(left)], axis=0).astype(bf16)
        right_x = jnp.concatenate([*split_three(right), jnp.zeros_like(right)], axis=0).astype(bf16)
        high = scalar_ref[part, 0]
        low = scalar_ref[part, 1]
        sums_i = lax.dot_general(
            jnp.concatenate([right_x, right_x], axis=1),
            jnp.concatenate([high, low], axis=1),
            (((1,), (1,)), ((), ())),
            preferred_element_type=f32,
        )
        sums_j = jnp.dot(
            jnp.concatenate([left_x, left_x], axis=1),
            jnp.concatenate([high, low], axis=0),
            preferred_element_type=f32,
        )
        sums_i = sums_i[0:8] + sums_i[8:16] + sums_i[16:24]
        sums_j = sums_j[0:8] + sums_j[8:16] + sums_j[16:24]
        row_sum[first] += left * sums_i[6:7] - sums_i
        col_sum[place] += right * sums_j[6:7] - sums_j

    def find(slot):
        first = pairs_ref[0, 0, 0, slot]
        second = pairs_ref[0, 0, 1, slot]
        owner = second >> 2
        tile = second & 3
        same = (owner == my_row) & (first == my_col * tiles_dev + tile)
        far = ((owner >> 2) & 1) ^ my_zh
        place = ((owner & 24) << 2) | ((owner & 3) << 3) | (far << 2) | tile
        owner = first >> 2
        first = (((owner & 1) ^ my_core) << 5) | ((owner >> 1) << 2) | (first & 3)
        return first, place, same

    def step(index, before):
        found = [find(index * UNROLL + part) for part in range(UNROLL)]
        any_same = functools.reduce(jnp.logical_or, [same for _, _, same in found])

        def work(masked):
            looked = []
            for part, (first, place, _) in enumerate(found):
                looked.append(features(first, place))
                add_forces(before[2 * part], before[2 * part + 1], part)
            for part, (_, _, same) in enumerate(found):
                scalars(looked[part], same if masked else None, part)

        @pl.when(any_same)
        def _():
            work(True)

        @pl.when(jnp.logical_not(any_same))
        def _():
            work(False)

        return tuple(place for first, second, _ in found for place in (first, second))

    last = lax.fori_loop(
        0, count_ref[0, 0] // UNROLL, step, tuple(jnp.int32(0) for _ in range(2 * UNROLL))
    )
    for part in range(UNROLL):
        add_forces(last[2 * part], last[2 * part + 1], part)

    def gather_owners(index, carry):
        for source, start, target in (
            (row_sum, 0, own_force),
            (row_sum, half_tiles, other_force),
            *((col_sum, part * half_tiles, col_force.at[part]) for part in range(4)),
        ):
            for axis in range(3):
                target[index, axis] = source[
                    pl.ds(start + index * tiles_dev, tiles_dev), axis, :
                ]
        return carry

    lax.fori_loop(0, own_force.shape[0], gather_owners, 0)


def shards(positions, vel_half, charges, types, six_table, twelve_table, tile_pairs, pair_counts):
    atoms_dev = positions.shape[1]
    tiles_dev = TILES_DEV
    n_row = X_SIZE * ZH_SIZE * Y_SIZE
    n_col = N_COL
    n_xy = X_SIZE * Y_SIZE
    n_zl = n_col // CORES
    n_z = ZH_SIZE * n_zl
    my_zh = (lax.axis_index("row") // Y_SIZE) % ZH_SIZE
    my_zl = lax.axis_index("col") // CORES
    xy_groups = [
        [(x * ZH_SIZE + zh) * Y_SIZE + y for x in range(X_SIZE) for y in range(Y_SIZE)]
        for zh in range(ZH_SIZE)
    ]
    z_groups = [
        [
            ((x * ZH_SIZE + zh) * Y_SIZE + y) * n_col + zl * CORES + core
            for zh in range(ZH_SIZE)
            for zl in range(n_zl)
        ]
        for x in range(X_SIZE)
        for y in range(Y_SIZE)
        for core in range(CORES)
    ]
    core_swap = [(at, at ^ 1) for at in range(n_col)]

    smem = pl.BlockSpec(memory_space=pltpu.SMEM)
    vmem = pl.BlockSpec(memory_space=pltpu.VMEM)
    moved_pos, block, blocks = pl.pallas_call(
        pack_kernel,
        out_shape=(
            jax.ShapeDtypeStruct((3, atoms_dev), jnp.float32),
            jax.ShapeDtypeStruct((CHANNELS, tiles_dev, LANES), jnp.float32),
            jax.ShapeDtypeStruct((n_z, CHANNELS, tiles_dev, LANES), jnp.float32),
        ),
        in_specs=[vmem] * 4,
        out_specs=(vmem, vmem, vmem),
        name="pack_atoms",
    )(
        positions,
        vel_half,
        charges.reshape(tiles_dev, TILE_ATOMS),
        types.reshape(tiles_dev, TILE_ATOMS),
    )
    pad = ((0, TYPE_ROWS - BEAD_TYPES), (0, TYPE_ROWS - BEAD_TYPES))
    six = jnp.pad(six_table.T * (6.0 / CUT_SQ**2), pad)
    twelve = jnp.pad(twelve_table.T * (12.0 / CUT_SQ**2), pad)
    parts = []
    for table in (six, twelve):
        upper = lax.reduce_precision(table, 8, 7)
        parts += [upper, table - upper]
    tables = jnp.concatenate(parts, axis=0).astype(jnp.bfloat16)

    z_blocks = lax.all_to_all(blocks, ("row", "col"), 0, 0, axis_index_groups=z_groups)
    z_blocks, tables = lax.optimization_barrier((z_blocks, tables))
    other_blocks = lax.ppermute(z_blocks, "col", core_swap)
    far_block = lax.dynamic_index_in_dim(z_blocks, (1 - my_zh) * n_zl + my_zl, 0, keepdims=False)
    both = jnp.stack([block, far_block], axis=0)
    col_blocks = lax.all_to_all(
        jnp.broadcast_to(both[None], (n_xy, ZH_SIZE, CHANNELS, tiles_dev, LANES)),
        "row",
        0,
        0,
        axis_index_groups=xy_groups,
    )
    row_tiles = n_col * tiles_dev
    col_tiles = n_row * tiles_dev
    row_block, left_factors = pl.pallas_call(
        row_kernel,
        out_shape=(
            jax.ShapeDtypeStruct((row_tiles, 8, LANES), jnp.float32),
            jax.ShapeDtypeStruct((row_tiles, TILE_ATOMS, LANES), jnp.bfloat16),
        ),
        in_specs=[vmem, vmem, vmem],
        out_specs=(vmem, vmem),
        compiler_params=pltpu.CompilerParams(vmem_limit_bytes=16 * 2**20),
        cost_estimate=pl.CostEstimate(
            flops=2 * row_tiles * 96 * 128 * 128, bytes_accessed=4 * 2**20, transcendentals=0
        ),
        name="row_factors",
    )(z_blocks, other_blocks, tables)
    own_force, other_force, col_force = pl.pallas_call(
        pair_kernel,
        out_shape=(
            jax.ShapeDtypeStruct((n_zl, 3, tiles_dev, LANES), jnp.float32),
            jax.ShapeDtypeStruct((n_zl, 3, tiles_dev, LANES), jnp.float32),
            jax.ShapeDtypeStruct((n_row // n_zl, n_zl, 3, tiles_dev, LANES), jnp.float32),
        ),
        in_specs=[smem, smem, vmem, vmem, vmem],
        out_specs=(vmem, vmem, vmem),
        scratch_shapes=[
            pltpu.VMEM((col_tiles, 8, LANES), jnp.float32),
            pltpu.VMEM((row_tiles, 8, LANES), jnp.float32),
            pltpu.VMEM((col_tiles, 8, LANES), jnp.float32),
            pltpu.VMEM((UNROLL, 2, TILE_ATOMS, LANES), jnp.bfloat16),
        ],
        compiler_params=pltpu.CompilerParams(vmem_limit_bytes=24 * 2**20),
        name="pair_forces",
    )(tile_pairs, pair_counts, row_block, left_factors, col_blocks.reshape(n_row, CHANNELS, tiles_dev, LANES))
    core_force = lax.ppermute(other_force, "col", core_swap)
    col_parts = lax.all_to_all(
        col_force.reshape(n_xy, ZH_SIZE, 3, tiles_dev, LANES),
        "row",
        0,
        0,
        axis_index_groups=xy_groups,
    )
    col_sum = jnp.sum(col_parts, axis=0)
    row_sum = own_force + core_force
    to_zh = lax.broadcasted_iota(jnp.int32, (ZH_SIZE, n_zl, 3, tiles_dev, LANES), 0)
    to_zl = lax.broadcasted_iota(jnp.int32, (ZH_SIZE, n_zl, 3, tiles_dev, LANES), 1)
    far_sum = jnp.where(to_zl == my_zl, col_sum[1][None, None], 0.0)
    z_parts = lax.all_to_all(
        jnp.where(to_zh == my_zh, row_sum[None], far_sum).reshape(n_z, 3, tiles_dev, LANES),
        ("row", "col"),
        0,
        0,
        axis_index_groups=z_groups,
    )
    force = jnp.sum(z_parts, axis=0) + col_sum[0]
    force_new = force.reshape(3, atoms_dev)
    velocity_new = vel_half + HALF_KICK * force_new
    return (moved_pos, force_new, velocity_new)


def solution(mesh):
    placed = (
        P(None, ("row", "col")),
        P(None, ("row", "col")),
        P(("row", "col")),
        P(("row", "col")),
        P(),
        P(),
        P("row", "col", None, None),
        P("row", "col"),
    )
    return jax.shard_map(
        shards,
        mesh=mesh,
        in_specs=placed,
        out_specs=(P(None, ("row", "col")), P(None, ("row", "col")), P(None, ("row", "col"))),
        check_vma=False,
    )
```

```python
import functools
import jax
import jax.numpy as jnp
from jax import lax
from jax.experimental import pallas as pl
from jax.experimental.pallas import tpu as pltpu
from jax.sharding import PartitionSpec as P

TILE_ATOMS = 128
TILES_DEV = 4
BEAD_TYPES = 18
LANES = 128

TIME_STEP = 0.02
HALF_KICK = 0.01 / 72.0
SOFT_CORE = 0.5
COULOMB = 9.262364
REACTION = 0.28935185
CUT_SQ = 1.44
CENTRE = 1.2

X_SIZE = 4
ZH_SIZE = 2
Y_SIZE = 4
N_COL = 16
CORES = 2
CHANNELS = 5
TYPE_ROWS = 24
UNROLL = 16
PREPARED = 16

def split_three(values):
    upper = values.astype(jnp.bfloat16).astype(jnp.float32)
    rest = values - upper
    middle = rest.astype(jnp.bfloat16).astype(jnp.float32)
    return upper, middle, rest - middle


def pack_kernel(positions_ref, vel_ref, charge_ref, type_ref, moved_ref, blocks_ref):
    moved = positions_ref[...] + TIME_STEP * vel_ref[...]
    moved_ref[...] = moved
    centred = moved - CENTRE
    channels = [
        jnp.concatenate(
            [
                centred[axis : axis + 1, tile * TILE_ATOMS : (tile + 1) * TILE_ATOMS]
                for tile in range(TILES_DEV)
            ],
            axis=0,
        )
        for axis in range(3)
    ]
    channels += [charge_ref[...], type_ref[...].astype(jnp.float32)]
    for channel, values in enumerate(channels):
        for copy in range(blocks_ref.shape[0]):
            blocks_ref[copy, channel] = values


def join_kernel(z_ref, blocks_ref, own_ref):
    n_zl = own_ref.shape[0]
    my_zh = (lax.axis_index("row") // Y_SIZE) % ZH_SIZE
    my_zl = lax.axis_index("col") // CORES
    for half, zh in enumerate((my_zh, 1 - my_zh)):
        block = z_ref[zh * n_zl + my_zl]
        for copy in range(blocks_ref.shape[0]):
            blocks_ref[copy, half] = block
    for owner in range(n_zl):
        own_ref[owner] = z_ref[my_zh * n_zl + owner]


def table_kernel(six_ref, twelve_ref, pairs_ref, count_ref, table_ref, list_ref):
    parts = []
    for table, factor in ((six_ref, 6.0), (twelve_ref, 12.0)):
        scaled = table[...] * (factor / CUT_SQ**2)
        upper = scaled.astype(jnp.bfloat16).astype(jnp.float32)
        parts += [upper, scaled - upper]
    table_ref[...] = jnp.concatenate(parts, axis=0).astype(jnp.bfloat16)
    list_ref[0:2] = pairs_ref[...]
    list_ref[2:3] = jnp.broadcast_to(count_ref[...], (1, list_ref.shape[1]))


def hot_types(block):
    type_rows = lax.broadcasted_iota(jnp.int32, (TYPE_ROWS, LANES), 0).astype(jnp.float32)
    return (jnp.broadcast_to(block[5:6], (TYPE_ROWS, LANES)) == type_rows).astype(jnp.float32)


def spread(source, owner, target, start):
    x, y, z, charge, kind = [source[owner, channel] for channel in range(CHANNELS)]
    one = jnp.ones_like(x)
    channels = (x, y, z, x * x + y * y + z * z, charge, kind, one, jnp.zeros_like(x))
    for channel, values in enumerate(channels):
        target[pl.ds(start, TILES_DEV), channel, :] = values


def row_kernel(own_ref, other_ref, table_ref, row_block, lhs_ref):
    f32 = jnp.float32
    half_tiles = row_block.shape[0] // CORES
    sub8 = lax.broadcasted_iota(jnp.int32, (8, LANES), 0)
    scale = jnp.where(sub8 < 3, -2.0, jnp.where(sub8 == 4, COULOMB / CUT_SQ**2, 0.0)).astype(f32)

    def spread_owners(index, carry):
        spread(own_ref, index, row_block, index * TILES_DEV)
        spread(other_ref, index, row_block, half_tiles + index * TILES_DEV)
        return carry

    lax.fori_loop(0, own_ref.shape[0], spread_owners, 0)

    def prepare(index, carry):
        wholes = []
        for part in range(PREPARED):
            block = row_block[index * PREPARED + part]
            left = block * scale
            left = jnp.where(sub8 == 3, 1.0, left)
            left = jnp.where(sub8 == 6, block[3:4] + SOFT_CORE, left)
            upper, middle, _ = split_three(left)
            coefs = jnp.dot(
                table_ref[...],
                hot_types(block).astype(jnp.bfloat16),
                preferred_element_type=f32,
            )
            wholes.append(jnp.concatenate([upper, upper, middle, middle, coefs], axis=0))
        for part in range(PREPARED):
            lhs_ref[index * PREPARED + part] = wholes[part].T.astype(jnp.bfloat16)
        return carry

    lax.fori_loop(0, row_block.shape[0] // PREPARED, prepare, 0)


def pair_kernel(
    pairs_ref, row_block, lhs_ref, col_ref,
    own_force, other_force, col_force,
    col_block, row_sum, col_sum, scalar_ref
):
    tiles_dev = TILES_DEV
    my_row = lax.axis_index("row")
    my_col = lax.axis_index("col")
    my_zh = (my_row // Y_SIZE) % ZH_SIZE
    my_core = my_col % CORES
    half_tiles = row_block.shape[0] // CORES
    f32 = jnp.float32
    bf16 = jnp.bfloat16
    sub8 = lax.broadcasted_iota(jnp.int32, (8, LANES), 0)
    sub8 = lax.broadcasted_iota(jnp.int32, (8, LANES), 0)
    lane = lax.broadcasted_iota(jnp.int32, (TILE_ATOMS, LANES), 1)

    row_sum[...] = jnp.zeros(row_sum.shape, f32)
    col_sum[...] = jnp.zeros(col_sum.shape, f32)
    scalar_ref[...] = jnp.zeros(scalar_ref.shape, bf16)

    def spread_owners(index, carry):
        for part in range(4):
            owner = index * 4 + part
            spread(col_ref, owner, col_block, owner * TILES_DEV)
        return carry

    lax.fori_loop(0, col_ref.shape[0] // 4, spread_owners, 0)

    def features(first, place):
        right = col_block[place]
        upper, middle, _ = split_three(right)
        hot = hot_types(right)
        zero = jnp.zeros_like(hot)
        dist = [jnp.where(sub8 == 4, 0.0, part) for part in (upper, middle)]
        charge = [jnp.where(sub8 == 4, part, 0.0) for part in (upper, middle)]
        none = jnp.zeros((32, LANES), f32)
        rhs = [
            jnp.concatenate([*dist, *dist, zero, zero, zero, zero], axis=0),
            jnp.concatenate([*charge, *charge, zero, zero, zero, zero], axis=0),
            jnp.concatenate([none, hot, hot, zero, zero], axis=0),
            jnp.concatenate([none, zero, zero, hot, hot], axis=0),
        ]
        left = lhs_ref[first]
        looked = []
        for which in (0, 2):
            both = jnp.concatenate(rhs[which : which + 2], axis=1).astype(bf16)
            product = jnp.dot(left, both, preferred_element_type=f32)
            looked += [product[:, 0:LANES], product[:, LANES:]]
        return looked

    def scalars(looked, same, part):
        soft_sq, charge, six, twelve = looked
        root = lax.rsqrt(soft_sq)
        inverse = root * root
        inverse_two = inverse * inverse
        inverse_four = inverse_two * inverse_two
        dispersion = inverse_four * (twelve * (inverse_two * inverse) - six)
        coulomb = charge * (inverse * root - 2.0 * REACTION)
        switch = jnp.maximum((CUT_SQ + SOFT_CORE) - soft_sq, 0.0)
        scalar = (dispersion + coulomb) * (switch * switch)
        if same is not None:
            at_i = lax.broadcasted_iota(jnp.int32, (TILE_ATOMS, LANES), 0)
            scalar = jnp.where((at_i < lane) | jnp.logical_not(same), scalar, 0.0)
        high = scalar.astype(bf16)
        scalar_ref[part, 0] = high
        scalar_ref[part, 1] = (scalar - high.astype(f32)).astype(bf16)

    def add_forces(first, place, part):
        left = row_block[first]
        right = col_block[place]
        left_x = jnp.concatenate([*split_three(left), jnp.zeros_like(left)], axis=0).astype(bf16)
        right_x = jnp.concatenate([*split_three(right), jnp.zeros_like(right)], axis=0).astype(bf16)
        high = scalar_ref[part, 0]
        low = scalar_ref[part, 1]
        sums_i = lax.dot_general(
            jnp.concatenate([right_x, right_x], axis=1),
            jnp.concatenate([high, low], axis=1),
            (((1,), (1,)), ((), ())),
            preferred_element_type=f32,
        )
        sums_j = jnp.dot(
            jnp.concatenate([left_x, left_x], axis=1),
            jnp.concatenate([high, low], axis=0),
            preferred_element_type=f32,
        )
        sums_i = sums_i[0:8] + sums_i[8:16] + sums_i[16:24]
        sums_j = sums_j[0:8] + sums_j[8:16] + sums_j[16:24]
        row_sum[first] += left * sums_i[6:7] - sums_i
        col_sum[place] += right * sums_j[6:7] - sums_j

    def find(slot):
        first = pairs_ref[0, slot]
        second = pairs_ref[1, slot]
        owner = second >> 2
        tile = second & 3
        same = (owner == my_row) & (first == my_col * tiles_dev + tile)
        far = ((owner >> 2) & 1) ^ my_zh
        place = ((owner & 24) << 2) | ((owner & 3) << 3) | (far << 2) | tile
        owner = first >> 2
        first = (((owner & 1) ^ my_core) << 5) | ((owner >> 1) << 2) | (first & 3)
        return first, place, same

    def step(index, before):
        found = [find(index * UNROLL + part) for part in range(UNROLL)]
        any_same = functools.reduce(jnp.logical_or, [same for _, _, same in found])

        def work(masked):
            looked = []
            for part, (first, place, _) in enumerate(found):
                looked.append(features(first, place))
                add_forces(before[2 * part], before[2 * part + 1], part)
            for part, (_, _, same) in enumerate(found):
                scalars(looked[part], same if masked else None, part)

        @pl.when(any_same)
        def _():
            work(True)

        @pl.when(jnp.logical_not(any_same))
        def _():
            work(False)

        return tuple(place for first, second, _ in found for place in (first, second))

    last = lax.fori_loop(
        0, pairs_ref[2, 0] // UNROLL, step, tuple(jnp.int32(0) for _ in range(2 * UNROLL))
    )
    for part in range(UNROLL):
        add_forces(last[2 * part], last[2 * part + 1], part)

    def gather_owners(index, carry):
        for source, start, target in (
            (row_sum, 0, own_force),
            (row_sum, half_tiles, other_force),
            *((col_sum, part * half_tiles, col_force.at[part]) for part in range(4)),
        ):
            for axis in range(3):
                target[index, axis] = source[
                    pl.ds(start + index * tiles_dev, tiles_dev), axis, :
                ]
        return carry

    lax.fori_loop(0, own_force.shape[0], gather_owners, 0)


def shards(positions, vel_half, charges, types, six_table, twelve_table, tile_pairs, pair_counts):
    atoms_dev = positions.shape[1]
    tiles_dev = TILES_DEV
    n_row = X_SIZE * ZH_SIZE * Y_SIZE
    n_col = N_COL
    n_xy = X_SIZE * Y_SIZE
    n_zl = n_col // CORES
    n_z = ZH_SIZE * n_zl
    my_zh = (lax.axis_index("row") >> 2) & 1
    my_zl = lax.axis_index("col") >> 1
    xy_groups = [
        [(x * ZH_SIZE + zh) * Y_SIZE + y for x in range(X_SIZE) for y in range(Y_SIZE)]
        for zh in range(ZH_SIZE)
    ]
    z_groups = [
        [
            ((x * ZH_SIZE + zh) * Y_SIZE + y) * n_col + zl * CORES + core
            for zh in range(ZH_SIZE)
            for zl in range(n_zl)
        ]
        for x in range(X_SIZE)
        for y in range(Y_SIZE)
        for core in range(CORES)
    ]
    core_swap = [(at, at ^ 1) for at in range(n_col)]

    smem = pl.BlockSpec(memory_space=pltpu.SMEM)
    vmem = pl.BlockSpec(memory_space=pltpu.VMEM)
    moved_pos, blocks = pl.pallas_call(
        pack_kernel,
        out_shape=(
            jax.ShapeDtypeStruct((3, atoms_dev), jnp.float32),
            jax.ShapeDtypeStruct((n_z, CHANNELS, tiles_dev, LANES), jnp.float32),
        ),
        in_specs=[vmem] * 4,
        out_specs=(vmem, vmem),
        name="pack_atoms",
    )(
        positions,
        vel_half,
        charges.reshape(tiles_dev, TILE_ATOMS),
        types.reshape(tiles_dev, TILE_ATOMS),
    )
    pad = ((0, TYPE_ROWS - BEAD_TYPES), (0, TYPE_ROWS - BEAD_TYPES))
    tables, pair_list = pl.pallas_call(
        table_kernel,
        out_shape=(
            jax.ShapeDtypeStruct((4 * TYPE_ROWS, TYPE_ROWS), jnp.bfloat16),
            jax.ShapeDtypeStruct((3, tile_pairs.shape[3]), jnp.int32),
        ),
        in_specs=[vmem] * 4,
        out_specs=(vmem, vmem),
        compiler_params=pltpu.CompilerParams(vmem_limit_bytes=4 * 2**20),
        name="tables",
    )(
        jnp.pad(six_table.T, pad),
        jnp.pad(twelve_table.T, pad),
        tile_pairs[0, 0],
        pair_counts,
    )
    z_blocks = lax.all_to_all(blocks, ("row", "col"), 0, 0, axis_index_groups=z_groups)
    z_blocks, tables, pair_list = lax.optimization_barrier((z_blocks, tables, pair_list))
    both, own_blocks = pl.pallas_call(
        join_kernel,
        out_shape=(
            jax.ShapeDtypeStruct((n_xy, ZH_SIZE, CHANNELS, tiles_dev, LANES), jnp.float32),
            jax.ShapeDtypeStruct((n_zl, CHANNELS, tiles_dev, LANES), jnp.float32),
        ),
        in_specs=[vmem],
        out_specs=(vmem, vmem),
        compiler_params=pltpu.CompilerParams(vmem_limit_bytes=4 * 2**20),
        name="join_halves",
    )(z_blocks)
    col_blocks = lax.all_to_all(both, "row", 0, 0, axis_index_groups=xy_groups)
    other_blocks = lax.ppermute(own_blocks, "col", core_swap)
    row_tiles = n_col * tiles_dev
    col_tiles = n_row * tiles_dev
    row_block, left_factors = pl.pallas_call(
        row_kernel,
        out_shape=(
            jax.ShapeDtypeStruct((row_tiles, 8, LANES), jnp.float32),
            jax.ShapeDtypeStruct((row_tiles, TILE_ATOMS, LANES), jnp.bfloat16),
        ),
        in_specs=[vmem, vmem, vmem],
        out_specs=(vmem, vmem),
        compiler_params=pltpu.CompilerParams(vmem_limit_bytes=16 * 2**20),
        cost_estimate=pl.CostEstimate(
            flops=2 * row_tiles * 96 * 128 * 128, bytes_accessed=4 * 2**20, transcendentals=0
        ),
        name="row_factors",
    )(own_blocks, other_blocks, tables)
    own_force, other_force, col_force = pl.pallas_call(
        pair_kernel,
        out_shape=(
            jax.ShapeDtypeStruct((n_zl, 3, tiles_dev, LANES), jnp.float32),
            jax.ShapeDtypeStruct((n_zl, 3, tiles_dev, LANES), jnp.float32),
            jax.ShapeDtypeStruct((n_row // n_zl, n_zl, 3, tiles_dev, LANES), jnp.float32),
        ),
        in_specs=[smem, vmem, vmem, vmem],
        out_specs=(vmem, vmem, vmem),
        scratch_shapes=[
            pltpu.VMEM((col_tiles, 8, LANES), jnp.float32),
            pltpu.VMEM((row_tiles, 8, LANES), jnp.float32),
            pltpu.VMEM((col_tiles, 8, LANES), jnp.float32),
            pltpu.VMEM((UNROLL, 2, TILE_ATOMS, LANES), jnp.bfloat16),
        ],
        compiler_params=pltpu.CompilerParams(vmem_limit_bytes=24 * 2**20),
        name="pair_forces",
    )(pair_list, row_block, left_factors, col_blocks.reshape(n_row, CHANNELS, tiles_dev, LANES))
    core_force = lax.ppermute(other_force, "col", core_swap)
    col_parts = lax.all_to_all(
        col_force.reshape(n_xy, ZH_SIZE, 3, tiles_dev, LANES),
        "row",
        0,
        0,
        axis_index_groups=xy_groups,
    )
    col_sum = jnp.sum(col_parts, axis=0)
    row_sum = own_force + core_force
    to_zh = lax.broadcasted_iota(jnp.int32, (ZH_SIZE, n_zl, 3, tiles_dev, LANES), 0)
    to_zl = lax.broadcasted_iota(jnp.int32, (ZH_SIZE, n_zl, 3, tiles_dev, LANES), 1)
    far_sum = jnp.where(to_zl == my_zl, col_sum[1][None, None], 0.0)
    z_parts = lax.all_to_all(
        jnp.where(to_zh == my_zh, row_sum[None], far_sum).reshape(n_z, 3, tiles_dev, LANES),
        ("row", "col"),
        0,
        0,
        axis_index_groups=z_groups,
    )
    force = jnp.sum(z_parts, axis=0) + col_sum[0]
    force_new = force.reshape(3, atoms_dev)
    velocity_new = vel_half + HALF_KICK * force_new
    return (moved_pos, force_new, velocity_new)


def solution(mesh):
    placed = (
        P(None, ("row", "col")),
        P(None, ("row", "col")),
        P(("row", "col")),
        P(("row", "col")),
        P(),
        P(),
        P("row", "col", None, None),
        P("row", "col"),
    )
    return jax.shard_map(
        shards,
        mesh=mesh,
        in_specs=placed,
        out_specs=(P(None, ("row", "col")), P(None, ("row", "col")), P(None, ("row", "col"))),
        check_vma=False,
    )
```

```python
import functools
import jax
import jax.numpy as jnp
from jax import lax
from jax.experimental import pallas as pl
from jax.experimental.pallas import tpu as pltpu
from jax.sharding import PartitionSpec as P

TILE_ATOMS = 128
TILES_DEV = 4
BEAD_TYPES = 18
LANES = 128

TIME_STEP = 0.02
HALF_KICK = 0.01 / 72.0
SOFT_CORE = 0.5
COULOMB = 9.262364
REACTION = 0.28935185
CUT_SQ = 1.44
CENTRE = 1.2

X_SIZE = 4
ZH_SIZE = 2
Y_SIZE = 4
N_COL = 16
CORES = 2
CHANNELS = 5
TYPE_ROWS = 24
UNROLL = 16
PREPARED = 32

def split_three(values):
    upper = values.astype(jnp.bfloat16).astype(jnp.float32)
    rest = values - upper
    middle = rest.astype(jnp.bfloat16).astype(jnp.float32)
    return upper, middle, rest - middle


def pack_kernel(positions_ref, vel_ref, charge_ref, type_ref, moved_ref, blocks_ref):
    moved = positions_ref[...] + TIME_STEP * vel_ref[...]
    moved_ref[...] = moved
    centred = moved - CENTRE
    channels = [
        jnp.concatenate(
            [
                centred[axis : axis + 1, tile * TILE_ATOMS : (tile + 1) * TILE_ATOMS]
                for tile in range(TILES_DEV)
            ],
            axis=0,
        )
        for axis in range(3)
    ]
    channels += [charge_ref[...], type_ref[...].astype(jnp.float32)]
    for channel, values in enumerate(channels):
        for copy in range(blocks_ref.shape[0]):
            blocks_ref[copy, channel] = values


def join_kernel(z_ref, blocks_ref, own_ref):
    n_zl = own_ref.shape[0]
    my_zh = (lax.axis_index("row") // Y_SIZE) % ZH_SIZE
    my_zl = lax.axis_index("col") // CORES
    for half, zh in enumerate((my_zh, 1 - my_zh)):
        block = z_ref[zh * n_zl + my_zl]
        for copy in range(blocks_ref.shape[0]):
            blocks_ref[copy, half] = block
    for owner in range(n_zl):
        own_ref[owner] = z_ref[my_zh * n_zl + owner]


def table_kernel(six_ref, twelve_ref, pairs_ref, count_ref, table_ref, list_ref):
    parts = []
    for table, factor in ((six_ref, 6.0), (twelve_ref, 12.0)):
        scaled = table[...] * (factor / CUT_SQ**2)
        upper = scaled.astype(jnp.bfloat16).astype(jnp.float32)
        parts += [upper, scaled - upper]
    table_ref[...] = jnp.concatenate(parts, axis=0).astype(jnp.bfloat16)
    list_ref[0:2] = pairs_ref[...]
    list_ref[2:3] = jnp.broadcast_to(count_ref[...], (1, list_ref.shape[1]))


def hot_types(block):
    type_rows = lax.broadcasted_iota(jnp.int32, (TYPE_ROWS, LANES), 0).astype(jnp.float32)
    return (jnp.broadcast_to(block[5:6], (TYPE_ROWS, LANES)) == type_rows).astype(jnp.float32)


def spread(source, owner, target, start):
    x, y, z, charge, kind = [source[owner, channel] for channel in range(CHANNELS)]
    one = jnp.ones_like(x)
    channels = (x, y, z, x * x + y * y + z * z, charge, kind, one, jnp.zeros_like(x))
    for channel, values in enumerate(channels):
        target[pl.ds(start, TILES_DEV), channel, :] = values


def row_kernel(own_ref, other_ref, table_ref, row_block, lhs_ref):
    f32 = jnp.float32
    half_tiles = row_block.shape[0] // CORES
    sub8 = lax.broadcasted_iota(jnp.int32, (8, LANES), 0)
    scale = jnp.where(sub8 < 3, -2.0, jnp.where(sub8 == 4, COULOMB / CUT_SQ**2, 0.0)).astype(f32)

    def spread_owners(index, carry):
        spread(own_ref, index, row_block, index * TILES_DEV)
        spread(other_ref, index, row_block, half_tiles + index * TILES_DEV)
        return carry

    lax.fori_loop(0, own_ref.shape[0], spread_owners, 0, unroll=True)

    def prepare(index, carry):
        wholes = []
        for part in range(PREPARED):
            block = row_block[index * PREPARED + part]
            left = block * scale
            left = jnp.where(sub8 == 3, 1.0, left)
            left = jnp.where(sub8 == 6, block[3:4] + SOFT_CORE, left)
            upper, middle, _ = split_three(left)
            coefs = jnp.dot(
                table_ref[...],
                hot_types(block).astype(jnp.bfloat16),
                preferred_element_type=f32,
            )
            wholes.append(jnp.concatenate([upper, upper, middle, middle, coefs], axis=0))
        for part in range(PREPARED):
            lhs_ref[index * PREPARED + part] = wholes[part].T.astype(jnp.bfloat16)
        return carry

    lax.fori_loop(0, row_block.shape[0] // PREPARED, prepare, 0)


def pair_kernel(
    pairs_ref, row_block, lhs_ref, col_ref,
    own_force, other_force, col_force,
    col_block, row_sum, col_sum, scalar_ref
):
    tiles_dev = TILES_DEV
    my_row = lax.axis_index("row")
    my_col = lax.axis_index("col")
    my_zh = (my_row // Y_SIZE) % ZH_SIZE
    my_core = my_col % CORES
    half_tiles = row_block.shape[0] // CORES
    f32 = jnp.float32
    bf16 = jnp.bfloat16
    sub8 = lax.broadcasted_iota(jnp.int32, (8, LANES), 0)
    sub8 = lax.broadcasted_iota(jnp.int32, (8, LANES), 0)
    lane = lax.broadcasted_iota(jnp.int32, (TILE_ATOMS, LANES), 1)

    row_sum[...] = jnp.zeros(row_sum.shape, f32)
    col_sum[...] = jnp.zeros(col_sum.shape, f32)
    scalar_ref[...] = jnp.zeros(scalar_ref.shape, bf16)

    def spread_owners(index, carry):
        for part in range(4):
            owner = index * 4 + part
            spread(col_ref, owner, col_block, owner * TILES_DEV)
        return carry

    lax.fori_loop(0, col_ref.shape[0] // 4, spread_owners, 0)

    def features(first, place):
        right = col_block[place]
        upper, middle, _ = split_three(right)
        hot = hot_types(right)
        zero = jnp.zeros_like(hot)
        dist = [jnp.where(sub8 == 4, 0.0, part) for part in (upper, middle)]
        charge = [jnp.where(sub8 == 4, part, 0.0) for part in (upper, middle)]
        none = jnp.zeros((32, LANES), f32)
        rhs = [
            jnp.concatenate([*dist, *dist, zero, zero, zero, zero], axis=0),
            jnp.concatenate([*charge, *charge, zero, zero, zero, zero], axis=0),
            jnp.concatenate([none, hot, hot, zero, zero], axis=0),
            jnp.concatenate([none, zero, zero, hot, hot], axis=0),
        ]
        left = lhs_ref[first]
        looked = []
        for which in (0, 2):
            both = jnp.concatenate(rhs[which : which + 2], axis=1).astype(bf16)
            product = jnp.dot(left, both, preferred_element_type=f32)
            looked += [product[:, 0:LANES], product[:, LANES:]]
        return looked

    def scalars(looked, same, part):
        soft_sq, charge, six, twelve = looked
        root = lax.rsqrt(soft_sq)
        inverse = root * root
        inverse_two = inverse * inverse
        inverse_four = inverse_two * inverse_two
        dispersion = inverse_four * (twelve * (inverse_two * inverse) - six)
        coulomb = charge * (inverse * root - 2.0 * REACTION)
        switch = jnp.maximum((CUT_SQ + SOFT_CORE) - soft_sq, 0.0)
        scalar = (dispersion + coulomb) * (switch * switch)
        if same is not None:
            at_i = lax.broadcasted_iota(jnp.int32, (TILE_ATOMS, LANES), 0)
            scalar = jnp.where((at_i < lane) | jnp.logical_not(same), scalar, 0.0)
        high = scalar.astype(bf16)
        scalar_ref[part, 0] = high
        scalar_ref[part, 1] = (scalar - high.astype(f32)).astype(bf16)

    def add_forces(first, place, part):
        left = row_block[first]
        right = col_block[place]
        left_x = jnp.concatenate([*split_three(left), jnp.zeros_like(left)], axis=0).astype(bf16)
        right_x = jnp.concatenate([*split_three(right), jnp.zeros_like(right)], axis=0).astype(bf16)
        high = scalar_ref[part, 0]
        low = scalar_ref[part, 1]
        sums_i = lax.dot_general(
            jnp.concatenate([right_x, right_x], axis=1),
            jnp.concatenate([high, low], axis=1),
            (((1,), (1,)), ((), ())),
            preferred_element_type=f32,
        )
        sums_j = jnp.dot(
            jnp.concatenate([left_x, left_x], axis=1),
            jnp.concatenate([high, low], axis=0),
            preferred_element_type=f32,
        )
        sums_i = sums_i[0:8] + sums_i[8:16] + sums_i[16:24]
        sums_j = sums_j[0:8] + sums_j[8:16] + sums_j[16:24]
        row_sum[first] += left * sums_i[6:7] - sums_i
        col_sum[place] += right * sums_j[6:7] - sums_j

    def find(slot):
        first = pairs_ref[0, slot]
        second = pairs_ref[1, slot]
        owner = second >> 2
        tile = second & 3
        same = (owner == my_row) & (first == my_col * tiles_dev + tile)
        far = ((owner >> 2) & 1) ^ my_zh
        place = ((owner & 24) << 2) | ((owner & 3) << 3) | (far << 2) | tile
        owner = first >> 2
        first = (((owner & 1) ^ my_core) << 5) | ((owner >> 1) << 2) | (first & 3)
        return first, place, same

    def step(index, before):
        found = [find(index * UNROLL + part) for part in range(UNROLL)]
        any_same = functools.reduce(jnp.logical_or, [same for _, _, same in found])

        def work(masked):
            looked = []
            for part, (first, place, _) in enumerate(found):
                looked.append(features(first, place))
                add_forces(before[2 * part], before[2 * part + 1], part)
            for part, (_, _, same) in enumerate(found):
                scalars(looked[part], same if masked else None, part)

        @pl.when(any_same)
        def _():
            work(True)

        @pl.when(jnp.logical_not(any_same))
        def _():
            work(False)

        return tuple(place for first, second, _ in found for place in (first, second))

    last = lax.fori_loop(
        0, pairs_ref[2, 0] // UNROLL, step, tuple(jnp.int32(0) for _ in range(2 * UNROLL))
    )
    for part in range(UNROLL):
        add_forces(last[2 * part], last[2 * part + 1], part)

    def gather_owners(index, carry):
        for source, start, target in (
            (row_sum, 0, own_force),
            (row_sum, half_tiles, other_force),
            *((col_sum, part * half_tiles, col_force.at[part]) for part in range(4)),
        ):
            for axis in range(3):
                target[index, axis] = source[
                    pl.ds(start + index * tiles_dev, tiles_dev), axis, :
                ]
        return carry

    lax.fori_loop(0, own_force.shape[0], gather_owners, 0, unroll=True)


def shards(positions, vel_half, charges, types, six_table, twelve_table, tile_pairs, pair_counts):
    atoms_dev = positions.shape[1]
    tiles_dev = TILES_DEV
    n_row = X_SIZE * ZH_SIZE * Y_SIZE
    n_col = N_COL
    n_xy = X_SIZE * Y_SIZE
    n_zl = n_col // CORES
    n_z = ZH_SIZE * n_zl
    my_zh = (lax.axis_index("row") >> 2) & 1
    my_zl = lax.axis_index("col") >> 1
    xy_groups = [
        [(x * ZH_SIZE + zh) * Y_SIZE + y for x in range(X_SIZE) for y in range(Y_SIZE)]
        for zh in range(ZH_SIZE)
    ]
    z_groups = [
        [
            ((x * ZH_SIZE + zh) * Y_SIZE + y) * n_col + zl * CORES + core
            for zh in range(ZH_SIZE)
            for zl in range(n_zl)
        ]
        for x in range(X_SIZE)
        for y in range(Y_SIZE)
        for core in range(CORES)
    ]
    core_swap = [(at, at ^ 1) for at in range(n_col)]

    smem = pl.BlockSpec(memory_space=pltpu.SMEM)
    vmem = pl.BlockSpec(memory_space=pltpu.VMEM)
    moved_pos, blocks = pl.pallas_call(
        pack_kernel,
        out_shape=(
            jax.ShapeDtypeStruct((3, atoms_dev), jnp.float32),
            jax.ShapeDtypeStruct((n_z, CHANNELS, tiles_dev, LANES), jnp.float32),
        ),
        in_specs=[vmem] * 4,
        out_specs=(vmem, vmem),
        name="pack_atoms",
    )(
        positions,
        vel_half,
        charges.reshape(tiles_dev, TILE_ATOMS),
        types.reshape(tiles_dev, TILE_ATOMS),
    )
    pad = ((0, TYPE_ROWS - BEAD_TYPES), (0, TYPE_ROWS - BEAD_TYPES))
    tables, pair_list = pl.pallas_call(
        table_kernel,
        out_shape=(
            jax.ShapeDtypeStruct((4 * TYPE_ROWS, TYPE_ROWS), jnp.bfloat16),
            jax.ShapeDtypeStruct((3, tile_pairs.shape[3]), jnp.int32),
        ),
        in_specs=[vmem] * 4,
        out_specs=(vmem, vmem),
        compiler_params=pltpu.CompilerParams(vmem_limit_bytes=4 * 2**20),
        name="tables",
    )(
        jnp.pad(six_table.T, pad),
        jnp.pad(twelve_table.T, pad),
        tile_pairs[0, 0],
        pair_counts,
    )
    z_blocks = lax.all_to_all(blocks, ("row", "col"), 0, 0, axis_index_groups=z_groups)
    z_blocks, tables, pair_list = lax.optimization_barrier((z_blocks, tables, pair_list))
    both, own_blocks = pl.pallas_call(
        join_kernel,
        out_shape=(
            jax.ShapeDtypeStruct((n_xy, ZH_SIZE, CHANNELS, tiles_dev, LANES), jnp.float32),
            jax.ShapeDtypeStruct((n_zl, CHANNELS, tiles_dev, LANES), jnp.float32),
        ),
        in_specs=[vmem],
        out_specs=(vmem, vmem),
        compiler_params=pltpu.CompilerParams(vmem_limit_bytes=4 * 2**20),
        name="join_halves",
    )(z_blocks)
    col_blocks = lax.all_to_all(both, "row", 0, 0, axis_index_groups=xy_groups)
    other_blocks = lax.ppermute(own_blocks, "col", core_swap)
    row_tiles = n_col * tiles_dev
    col_tiles = n_row * tiles_dev
    row_block, left_factors = pl.pallas_call(
        row_kernel,
        out_shape=(
            jax.ShapeDtypeStruct((row_tiles, 8, LANES), jnp.float32),
            jax.ShapeDtypeStruct((row_tiles, TILE_ATOMS, LANES), jnp.bfloat16),
        ),
        in_specs=[vmem, vmem, vmem],
        out_specs=(vmem, vmem),
        compiler_params=pltpu.CompilerParams(vmem_limit_bytes=16 * 2**20),
        cost_estimate=pl.CostEstimate(
            flops=2 * row_tiles * 96 * 128 * 128, bytes_accessed=4 * 2**20, transcendentals=0
        ),
        name="row_factors",
    )(own_blocks, other_blocks, tables)
    own_force, other_force, col_force = pl.pallas_call(
        pair_kernel,
        out_shape=(
            jax.ShapeDtypeStruct((n_zl, 3, tiles_dev, LANES), jnp.float32),
            jax.ShapeDtypeStruct((n_zl, 3, tiles_dev, LANES), jnp.float32),
            jax.ShapeDtypeStruct((n_row // n_zl, n_zl, 3, tiles_dev, LANES), jnp.float32),
        ),
        in_specs=[smem, vmem, vmem, vmem],
        out_specs=(vmem, vmem, vmem),
        scratch_shapes=[
            pltpu.VMEM((col_tiles, 8, LANES), jnp.float32),
            pltpu.VMEM((row_tiles, 8, LANES), jnp.float32),
            pltpu.VMEM((col_tiles, 8, LANES), jnp.float32),
            pltpu.VMEM((UNROLL, 2, TILE_ATOMS, LANES), jnp.bfloat16),
        ],
        compiler_params=pltpu.CompilerParams(vmem_limit_bytes=24 * 2**20),
        name="pair_forces",
    )(pair_list, row_block, left_factors, col_blocks.reshape(n_row, CHANNELS, tiles_dev, LANES))
    core_force = lax.ppermute(other_force, "col", core_swap)
    col_parts = lax.all_to_all(
        col_force.reshape(n_xy, ZH_SIZE, 3, tiles_dev, LANES),
        "row",
        0,
        0,
        axis_index_groups=xy_groups,
    )
    col_sum = jnp.sum(col_parts, axis=0)
    row_sum = own_force + core_force
    to_zh = lax.broadcasted_iota(jnp.int32, (ZH_SIZE, n_zl, 3, tiles_dev, LANES), 0)
    to_zl = lax.broadcasted_iota(jnp.int32, (ZH_SIZE, n_zl, 3, tiles_dev, LANES), 1)
    far_sum = jnp.where(to_zl == my_zl, col_sum[1][None, None], 0.0)
    z_parts = lax.all_to_all(
        jnp.where(to_zh == my_zh, row_sum[None], far_sum).reshape(n_z, 3, tiles_dev, LANES),
        ("row", "col"),
        0,
        0,
        axis_index_groups=z_groups,
    )
    force = jnp.sum(z_parts, axis=0) + col_sum[0]
    force_new = force.reshape(3, atoms_dev)
    velocity_new = vel_half + HALF_KICK * force_new
    return (moved_pos, force_new, velocity_new)


def solution(mesh):
    placed = (
        P(None, ("row", "col")),
        P(None, ("row", "col")),
        P(("row", "col")),
        P(("row", "col")),
        P(),
        P(),
        P("row", "col", None, None),
        P("row", "col"),
    )
    return jax.shard_map(
        shards,
        mesh=mesh,
        in_specs=placed,
        out_specs=(P(None, ("row", "col")), P(None, ("row", "col")), P(None, ("row", "col"))),
        check_vma=False,
    )
```

```python
import jax
import jax.numpy as jnp
from jax import lax
from jax.experimental import pallas as pl
from jax.experimental.pallas import tpu as pltpu
from jax.sharding import PartitionSpec as P

TILE_ATOMS = 128
TILES_DEV = 4
BEAD_TYPES = 18
LANES = 128

TIME_STEP = 0.02
HALF_KICK = 0.01 / 72.0
SOFT_CORE = 0.5
COULOMB = 9.262364
REACTION = 0.28935185
CUT_SQ = 1.44
CENTRE = 1.2

X_SIZE = 4
ZH_SIZE = 2
Y_SIZE = 4
N_COL = 16
CORES = 2
CHANNELS = 5
TYPE_ROWS = 24
UNROLL = 16
LAG = 8
PREPARED = 32

def split_three(values):
    upper = values.astype(jnp.bfloat16).astype(jnp.float32)
    rest = values - upper
    middle = rest.astype(jnp.bfloat16).astype(jnp.float32)
    return upper, middle, rest - middle


def pack_kernel(positions_ref, vel_ref, charge_ref, type_ref, moved_ref, blocks_ref):
    moved = positions_ref[...] + TIME_STEP * vel_ref[...]
    moved_ref[...] = moved
    centred = moved - CENTRE
    channels = [
        jnp.concatenate(
            [
                centred[axis : axis + 1, tile * TILE_ATOMS : (tile + 1) * TILE_ATOMS]
                for tile in range(TILES_DEV)
            ],
            axis=0,
        )
        for axis in range(3)
    ]
    channels += [charge_ref[...], type_ref[...].astype(jnp.float32)]
    for channel, values in enumerate(channels):
        for copy in range(blocks_ref.shape[0]):
            blocks_ref[copy, channel] = values


def join_kernel(z_ref, blocks_ref, own_ref):
    n_zl = own_ref.shape[0]
    my_zh = (lax.axis_index("row") // Y_SIZE) % ZH_SIZE
    my_zl = lax.axis_index("col") // CORES
    for half, zh in enumerate((my_zh, 1 - my_zh)):
        block = z_ref[zh * n_zl + my_zl]
        for copy in range(blocks_ref.shape[0]):
            blocks_ref[copy, half] = block
    for owner in range(n_zl):
        own_ref[owner] = z_ref[my_zh * n_zl + owner]


def table_kernel(six_ref, twelve_ref, pairs_ref, count_ref, table_ref, list_ref):
    parts = []
    for table, factor in ((six_ref, 6.0), (twelve_ref, 12.0)):
        scaled = table[...] * (factor / CUT_SQ**2)
        upper = scaled.astype(jnp.bfloat16).astype(jnp.float32)
        parts += [upper, scaled - upper]
    table_ref[...] = jnp.concatenate(parts, axis=0).astype(jnp.bfloat16)
    list_ref[0:2] = pairs_ref[...]
    list_ref[2:3] = jnp.broadcast_to(count_ref[...], (1, list_ref.shape[1]))


def hot_types(block):
    type_rows = lax.broadcasted_iota(jnp.int32, (TYPE_ROWS, LANES), 0).astype(jnp.float32)
    return (jnp.broadcast_to(block[5:6], (TYPE_ROWS, LANES)) == type_rows).astype(jnp.float32)


def spread(source, owner, target, start):
    x, y, z, charge, kind = [source[owner, channel] for channel in range(CHANNELS)]
    one = jnp.ones_like(x)
    channels = (x, y, z, x * x + y * y + z * z, charge, kind, one, jnp.zeros_like(x))
    for channel, values in enumerate(channels):
        target[pl.ds(start, TILES_DEV), channel, :] = values


def row_kernel(own_ref, other_ref, table_ref, row_block, lhs_ref):
    f32 = jnp.float32
    half_tiles = row_block.shape[0] // CORES
    sub8 = lax.broadcasted_iota(jnp.int32, (8, LANES), 0)
    scale = jnp.where(sub8 < 3, -2.0, jnp.where(sub8 == 4, COULOMB / CUT_SQ**2, 0.0)).astype(f32)

    def spread_owners(index, carry):
        spread(own_ref, index, row_block, index * TILES_DEV)
        spread(other_ref, index, row_block, half_tiles + index * TILES_DEV)
        return carry

    lax.fori_loop(0, own_ref.shape[0], spread_owners, 0, unroll=True)

    def prepare(index, carry):
        wholes = []
        for part in range(PREPARED):
            block = row_block[index * PREPARED + part]
            left = block * scale
            left = jnp.where(sub8 == 3, 1.0, left)
            left = jnp.where(sub8 == 6, block[3:4] + SOFT_CORE, left)
            upper, middle, _ = split_three(left)
            coefs = jnp.dot(
                table_ref[...],
                hot_types(block).astype(jnp.bfloat16),
                preferred_element_type=f32,
            )
            wholes.append(jnp.concatenate([upper, upper, middle, middle, coefs], axis=0))
        for part in range(PREPARED):
            lhs_ref[index * PREPARED + part] = wholes[part].T.astype(jnp.bfloat16)
        return carry

    lax.fori_loop(0, row_block.shape[0] // PREPARED, prepare, 0)


def pair_kernel(
    pairs_ref, row_block, lhs_ref, col_ref,
    own_force, other_force, col_force,
    col_block, row_sum, col_sum, scalar_ref
):
    tiles_dev = TILES_DEV
    my_row = lax.axis_index("row")
    my_col = lax.axis_index("col")
    my_zh = (my_row // Y_SIZE) % ZH_SIZE
    my_core = my_col % CORES
    half_tiles = row_block.shape[0] // CORES
    f32 = jnp.float32
    bf16 = jnp.bfloat16
    sub8 = lax.broadcasted_iota(jnp.int32, (8, LANES), 0)
    sub8 = lax.broadcasted_iota(jnp.int32, (8, LANES), 0)
    lane = lax.broadcasted_iota(jnp.int32, (TILE_ATOMS, LANES), 1)

    row_sum[...] = jnp.zeros(row_sum.shape, f32)
    col_sum[...] = jnp.zeros(col_sum.shape, f32)
    scalar_ref[...] = jnp.zeros(scalar_ref.shape, bf16)

    def spread_owners(index, carry):
        for part in range(4):
            owner = index * 4 + part
            spread(col_ref, owner, col_block, owner * TILES_DEV)
        return carry

    lax.fori_loop(0, col_ref.shape[0] // 4, spread_owners, 0)

    def features(first, place):
        right = col_block[place]
        upper, middle, _ = split_three(right)
        hot = hot_types(right)
        zero = jnp.zeros_like(hot)
        dist = [jnp.where(sub8 == 4, 0.0, part) for part in (upper, middle)]
        charge = [jnp.where(sub8 == 4, part, 0.0) for part in (upper, middle)]
        none = jnp.zeros((32, LANES), f32)
        rhs = [
            jnp.concatenate([*dist, *dist, zero, zero, zero, zero], axis=0),
            jnp.concatenate([*charge, *charge, zero, zero, zero, zero], axis=0),
            jnp.concatenate([none, hot, hot, zero, zero], axis=0),
            jnp.concatenate([none, zero, zero, hot, hot], axis=0),
        ]
        left = lhs_ref[first]
        looked = []
        for which in (0, 2):
            both = jnp.concatenate(rhs[which : which + 2], axis=1).astype(bf16)
            product = jnp.dot(left, both, preferred_element_type=f32)
            looked += [product[:, 0:LANES], product[:, LANES:]]
        return looked

    def scalars(looked, same, part):
        soft_sq, charge, six, twelve = looked
        root = lax.rsqrt(soft_sq)
        inverse = root * root
        inverse_two = inverse * inverse
        inverse_four = inverse_two * inverse_two
        dispersion = inverse_four * (twelve * (inverse_two * inverse) - six)
        coulomb = charge * (inverse * root - 2.0 * REACTION)
        switch = jnp.maximum((CUT_SQ + SOFT_CORE) - soft_sq, 0.0)
        scalar = (dispersion + coulomb) * (switch * switch)
        at_i = lax.broadcasted_iota(jnp.int32, (TILE_ATOMS, LANES), 0)
        scalar = jnp.where((at_i < lane) | jnp.logical_not(same), scalar, 0.0)
        high = scalar.astype(bf16)
        scalar_ref[part, 0] = high
        scalar_ref[part, 1] = (scalar - high.astype(f32)).astype(bf16)

    def add_forces(first, place, part):
        left = row_block[first]
        right = col_block[place]
        left_x = jnp.concatenate([*split_three(left), jnp.zeros_like(left)], axis=0).astype(bf16)
        right_x = jnp.concatenate([*split_three(right), jnp.zeros_like(right)], axis=0).astype(bf16)
        high = scalar_ref[part, 0]
        low = scalar_ref[part, 1]
        sums_i = lax.dot_general(
            jnp.concatenate([right_x, right_x], axis=1),
            jnp.concatenate([high, low], axis=1),
            (((1,), (1,)), ((), ())),
            preferred_element_type=f32,
        )
        sums_j = jnp.dot(
            jnp.concatenate([left_x, left_x], axis=1),
            jnp.concatenate([high, low], axis=0),
            preferred_element_type=f32,
        )
        sums_i = sums_i[0:8] + sums_i[8:16] + sums_i[16:24]
        sums_j = sums_j[0:8] + sums_j[8:16] + sums_j[16:24]
        row_sum[first] += left * sums_i[6:7] - sums_i
        col_sum[place] += right * sums_j[6:7] - sums_j

    def find(slot):
        first = pairs_ref[0, slot]
        second = pairs_ref[1, slot]
        owner = second >> 2
        tile = second & 3
        same = (owner == my_row) & (first == my_col * tiles_dev + tile)
        far = ((owner >> 2) & 1) ^ my_zh
        place = ((owner & 24) << 2) | ((owner & 3) << 3) | (far << 2) | tile
        owner = first >> 2
        first = (((owner & 1) ^ my_core) << 5) | ((owner >> 1) << 2) | (first & 3)
        return first, place, same

    def step(index, before):
        found = [find(index * UNROLL + part) for part in range(UNROLL)]
        for start in range(0, UNROLL, LAG):
            looked = []
            for part in range(start, start + LAG):
                looked.append(features(*found[part][:2]))
                if part < LAG:
                    add_forces(before[2 * part], before[2 * part + 1], UNROLL - LAG + part)
                else:
                    add_forces(*found[part - LAG][:2], part - LAG)
            for part in range(start, start + LAG):
                scalars(looked[part - start], found[part][2], part)
        return tuple(place for first, second, _ in found[-LAG:] for place in (first, second))

    last = lax.fori_loop(
        0, pairs_ref[2, 0] // UNROLL, step, tuple(jnp.int32(0) for _ in range(2 * LAG))
    )
    for part in range(LAG):
        add_forces(last[2 * part], last[2 * part + 1], UNROLL - LAG + part)

    def gather_owners(index, carry):
        for source, start, target in (
            (row_sum, 0, own_force),
            (row_sum, half_tiles, other_force),
            *((col_sum, part * half_tiles, col_force.at[part]) for part in range(4)),
        ):
            for axis in range(3):
                target[index, axis] = source[
                    pl.ds(start + index * tiles_dev, tiles_dev), axis, :
                ]
        return carry

    lax.fori_loop(0, own_force.shape[0], gather_owners, 0, unroll=True)


def shards(positions, vel_half, charges, types, six_table, twelve_table, tile_pairs, pair_counts):
    atoms_dev = positions.shape[1]
    tiles_dev = TILES_DEV
    n_row = X_SIZE * ZH_SIZE * Y_SIZE
    n_col = N_COL
    n_xy = X_SIZE * Y_SIZE
    n_zl = n_col // CORES
    n_z = ZH_SIZE * n_zl
    my_zh = (lax.axis_index("row") >> 2) & 1
    my_zl = lax.axis_index("col") >> 1
    xy_groups = [
        [(x * ZH_SIZE + zh) * Y_SIZE + y for x in range(X_SIZE) for y in range(Y_SIZE)]
        for zh in range(ZH_SIZE)
    ]
    z_groups = [
        [
            ((x * ZH_SIZE + zh) * Y_SIZE + y) * n_col + zl * CORES + core
            for zh in range(ZH_SIZE)
            for zl in range(n_zl)
        ]
        for x in range(X_SIZE)
        for y in range(Y_SIZE)
        for core in range(CORES)
    ]
    core_swap = [(at, at ^ 1) for at in range(n_col)]

    smem = pl.BlockSpec(memory_space=pltpu.SMEM)
    vmem = pl.BlockSpec(memory_space=pltpu.VMEM)
    moved_pos, blocks = pl.pallas_call(
        pack_kernel,
        out_shape=(
            jax.ShapeDtypeStruct((3, atoms_dev), jnp.float32),
            jax.ShapeDtypeStruct((n_z, CHANNELS, tiles_dev, LANES), jnp.float32),
        ),
        in_specs=[vmem] * 4,
        out_specs=(vmem, vmem),
        name="pack_atoms",
    )(
        positions,
        vel_half,
        charges.reshape(tiles_dev, TILE_ATOMS),
        types.reshape(tiles_dev, TILE_ATOMS),
    )
    pad = ((0, TYPE_ROWS - BEAD_TYPES), (0, TYPE_ROWS - BEAD_TYPES))
    tables, pair_list = pl.pallas_call(
        table_kernel,
        out_shape=(
            jax.ShapeDtypeStruct((4 * TYPE_ROWS, TYPE_ROWS), jnp.bfloat16),
            jax.ShapeDtypeStruct((3, tile_pairs.shape[3]), jnp.int32),
        ),
        in_specs=[vmem] * 4,
        out_specs=(vmem, vmem),
        compiler_params=pltpu.CompilerParams(vmem_limit_bytes=4 * 2**20),
        name="tables",
    )(
        jnp.pad(six_table.T, pad),
        jnp.pad(twelve_table.T, pad),
        tile_pairs[0, 0],
        pair_counts,
    )
    z_blocks = lax.all_to_all(blocks, ("row", "col"), 0, 0, axis_index_groups=z_groups)
    z_blocks, tables, pair_list = lax.optimization_barrier((z_blocks, tables, pair_list))
    both, own_blocks = pl.pallas_call(
        join_kernel,
        out_shape=(
            jax.ShapeDtypeStruct((n_xy, ZH_SIZE, CHANNELS, tiles_dev, LANES), jnp.float32),
            jax.ShapeDtypeStruct((n_zl, CHANNELS, tiles_dev, LANES), jnp.float32),
        ),
        in_specs=[vmem],
        out_specs=(vmem, vmem),
        compiler_params=pltpu.CompilerParams(vmem_limit_bytes=4 * 2**20),
        name="join_halves",
    )(z_blocks)
    col_blocks = lax.all_to_all(both, "row", 0, 0, axis_index_groups=xy_groups)
    other_blocks = lax.ppermute(own_blocks, "col", core_swap)
    row_tiles = n_col * tiles_dev
    col_tiles = n_row * tiles_dev
    row_block, left_factors = pl.pallas_call(
        row_kernel,
        out_shape=(
            jax.ShapeDtypeStruct((row_tiles, 8, LANES), jnp.float32),
            jax.ShapeDtypeStruct((row_tiles, TILE_ATOMS, LANES), jnp.bfloat16),
        ),
        in_specs=[vmem, vmem, vmem],
        out_specs=(vmem, vmem),
        compiler_params=pltpu.CompilerParams(vmem_limit_bytes=16 * 2**20),
        cost_estimate=pl.CostEstimate(
            flops=2 * row_tiles * 96 * 128 * 128, bytes_accessed=4 * 2**20, transcendentals=0
        ),
        name="row_factors",
    )(own_blocks, other_blocks, tables)
    own_force, other_force, col_force = pl.pallas_call(
        pair_kernel,
        out_shape=(
            jax.ShapeDtypeStruct((n_zl, 3, tiles_dev, LANES), jnp.float32),
            jax.ShapeDtypeStruct((n_zl, 3, tiles_dev, LANES), jnp.float32),
            jax.ShapeDtypeStruct((n_row // n_zl, n_zl, 3, tiles_dev, LANES), jnp.float32),
        ),
        in_specs=[smem, vmem, vmem, vmem],
        out_specs=(vmem, vmem, vmem),
        scratch_shapes=[
            pltpu.VMEM((col_tiles, 8, LANES), jnp.float32),
            pltpu.VMEM((row_tiles, 8, LANES), jnp.float32),
            pltpu.VMEM((col_tiles, 8, LANES), jnp.float32),
            pltpu.VMEM((UNROLL, 2, TILE_ATOMS, LANES), jnp.bfloat16),
        ],
        compiler_params=pltpu.CompilerParams(vmem_limit_bytes=24 * 2**20),
        name="pair_forces",
    )(pair_list, row_block, left_factors, col_blocks.reshape(n_row, CHANNELS, tiles_dev, LANES))
    core_force = lax.ppermute(other_force, "col", core_swap)
    col_parts = lax.all_to_all(
        col_force.reshape(n_xy, ZH_SIZE, 3, tiles_dev, LANES),
        "row",
        0,
        0,
        axis_index_groups=xy_groups,
    )
    col_sum = jnp.sum(col_parts, axis=0)
    row_sum = own_force + core_force
    to_zh = lax.broadcasted_iota(jnp.int32, (ZH_SIZE, n_zl, 3, tiles_dev, LANES), 0)
    to_zl = lax.broadcasted_iota(jnp.int32, (ZH_SIZE, n_zl, 3, tiles_dev, LANES), 1)
    far_sum = jnp.where(to_zl == my_zl, col_sum[1][None, None], 0.0)
    z_parts = lax.all_to_all(
        jnp.where(to_zh == my_zh, row_sum[None], far_sum).reshape(n_z, 3, tiles_dev, LANES),
        ("row", "col"),
        0,
        0,
        axis_index_groups=z_groups,
    )
    force = jnp.sum(z_parts, axis=0) + col_sum[0]
    force_new = force.reshape(3, atoms_dev)
    velocity_new = vel_half + HALF_KICK * force_new
    return (moved_pos, force_new, velocity_new)


def solution(mesh):
    placed = (
        P(None, ("row", "col")),
        P(None, ("row", "col")),
        P(("row", "col")),
        P(("row", "col")),
        P(),
        P(),
        P("row", "col", None, None),
        P("row", "col"),
    )
    return jax.shard_map(
        shards,
        mesh=mesh,
        in_specs=placed,
        out_specs=(P(None, ("row", "col")), P(None, ("row", "col")), P(None, ("row", "col"))),
        check_vma=False,
    )
```

```python
import jax
import jax.numpy as jnp
from jax import lax
from jax.experimental import pallas as pl
from jax.experimental.pallas import tpu as pltpu
from jax.sharding import PartitionSpec as P

TILE_ATOMS = 128
TILES_DEV = 4
BEAD_TYPES = 18
LANES = 128

TIME_STEP = 0.02
HALF_KICK = 0.01 / 72.0
SOFT_CORE = 0.5
COULOMB = 9.262364
REACTION = 0.28935185
CUT_SQ = 1.44
CENTRE = 1.2

X_SIZE = 4
ZH_SIZE = 2
Y_SIZE = 4
N_COL = 16
CORES = 2
CHANNELS = 5
TYPE_ROWS = 24
UNROLL = 16
LAG = 8
PREPARED = 32

def split_three(values):
    upper = values.astype(jnp.bfloat16).astype(jnp.float32)
    rest = values - upper
    middle = rest.astype(jnp.bfloat16).astype(jnp.float32)
    return upper, middle, rest - middle


def pack_kernel(positions_ref, vel_ref, charge_ref, type_ref, moved_ref, blocks_ref):
    moved = positions_ref[...] + TIME_STEP * vel_ref[...]
    moved_ref[...] = moved
    centred = moved - CENTRE
    channels = [
        jnp.concatenate(
            [
                centred[axis : axis + 1, tile * TILE_ATOMS : (tile + 1) * TILE_ATOMS]
                for tile in range(TILES_DEV)
            ],
            axis=0,
        )
        for axis in range(3)
    ]
    channels += [charge_ref[...], type_ref[...].astype(jnp.float32)]
    for channel, values in enumerate(channels):
        for copy in range(blocks_ref.shape[0]):
            blocks_ref[copy, channel] = values


def join_kernel(z_ref, blocks_ref, own_ref):
    n_zl = own_ref.shape[0]
    my_zh = (lax.axis_index("row") // Y_SIZE) % ZH_SIZE
    my_zl = lax.axis_index("col") // CORES
    for half, zh in enumerate((my_zh, 1 - my_zh)):
        block = z_ref[zh * n_zl + my_zl]
        for copy in range(blocks_ref.shape[0]):
            blocks_ref[copy, half] = block
    for owner in range(n_zl):
        own_ref[owner] = z_ref[my_zh * n_zl + owner]


def table_kernel(six_ref, twelve_ref, pairs_ref, count_ref, table_ref, list_ref):
    parts = []
    for table, factor in ((six_ref, 6.0), (twelve_ref, 12.0)):
        scaled = table[...] * (factor / CUT_SQ**2)
        upper = scaled.astype(jnp.bfloat16).astype(jnp.float32)
        parts += [upper, scaled - upper]
    table_ref[...] = jnp.concatenate(parts, axis=0).astype(jnp.bfloat16)
    list_ref[0:2] = pairs_ref[...]
    list_ref[2:3] = jnp.broadcast_to(count_ref[...], (1, list_ref.shape[1]))


def hot_types(block):
    type_rows = lax.broadcasted_iota(jnp.int32, (TYPE_ROWS, LANES), 0).astype(jnp.float32)
    return (jnp.broadcast_to(block[5:6], (TYPE_ROWS, LANES)) == type_rows).astype(jnp.float32)


def spread(source, owner, target, start):
    x, y, z, charge, kind = [source[owner, channel] for channel in range(CHANNELS)]
    one = jnp.ones_like(x)
    channels = (x, y, z, x * x + y * y + z * z, charge, kind, one, jnp.zeros_like(x))
    for channel, values in enumerate(channels):
        target[pl.ds(start, TILES_DEV), channel, :] = values


def row_kernel(own_ref, other_ref, table_ref, row_block, lhs_ref):
    f32 = jnp.float32
    half_tiles = row_block.shape[0] // CORES
    sub8 = lax.broadcasted_iota(jnp.int32, (8, LANES), 0)
    scale = jnp.where(sub8 < 3, -2.0, jnp.where(sub8 == 4, COULOMB / CUT_SQ**2, 0.0)).astype(f32)

    def spread_owners(index, carry):
        spread(own_ref, index, row_block, index * TILES_DEV)
        spread(other_ref, index, row_block, half_tiles + index * TILES_DEV)
        return carry

    lax.fori_loop(0, own_ref.shape[0], spread_owners, 0, unroll=True)

    def prepare(index, carry):
        wholes = []
        for part in range(PREPARED):
            block = row_block[index * PREPARED + part]
            left = block * scale
            left = jnp.where(sub8 == 3, 1.0, left)
            left = jnp.where(sub8 == 6, block[3:4] + SOFT_CORE, left)
            upper, middle, _ = split_three(left)
            coefs = jnp.dot(
                table_ref[...],
                hot_types(block).astype(jnp.bfloat16),
                preferred_element_type=f32,
            )
            wholes.append(jnp.concatenate([upper, upper, middle, middle, coefs], axis=0))
        for part in range(PREPARED):
            lhs_ref[index * PREPARED + part] = wholes[part].T.astype(jnp.bfloat16)
        return carry

    lax.fori_loop(0, row_block.shape[0] // PREPARED, prepare, 0)


def pair_kernel(
    pairs_ref, row_block, lhs_ref, col_ref,
    own_force, other_force, col_force,
    col_block, row_sum, col_sum, scalar_ref
):
    tiles_dev = TILES_DEV
    my_row = lax.axis_index("row")
    my_col = lax.axis_index("col")
    my_zh = (my_row // Y_SIZE) % ZH_SIZE
    my_core = my_col % CORES
    half_tiles = row_block.shape[0] // CORES
    f32 = jnp.float32
    bf16 = jnp.bfloat16
    sub8 = lax.broadcasted_iota(jnp.int32, (8, LANES), 0)
    sub8 = lax.broadcasted_iota(jnp.int32, (8, LANES), 0)
    shape = (TILE_ATOMS, LANES)
    ahead = lax.broadcasted_iota(jnp.int32, shape, 1) - lax.broadcasted_iota(jnp.int32, shape, 0)

    row_sum[...] = jnp.zeros(row_sum.shape, f32)
    col_sum[...] = jnp.zeros(col_sum.shape, f32)
    scalar_ref[UNROLL - LAG :] = jnp.zeros((LAG, *scalar_ref.shape[1:]), bf16)

    def spread_owners(index, carry):
        for part in range(4):
            owner = index * 4 + part
            spread(col_ref, owner, col_block, owner * TILES_DEV)
        return carry

    lax.fori_loop(0, col_ref.shape[0] // 4, spread_owners, 0)

    def features(first, place):
        right = col_block[place]
        upper, middle, _ = split_three(right)
        hot = hot_types(right)
        zero = jnp.zeros_like(hot)
        dist = [jnp.where(sub8 == 4, 0.0, part) for part in (upper, middle)]
        charge = [jnp.where(sub8 == 4, part, 0.0) for part in (upper, middle)]
        none = jnp.zeros((32, LANES), f32)
        rhs = [
            jnp.concatenate([*dist, *dist, zero, zero, zero, zero], axis=0),
            jnp.concatenate([*charge, *charge, zero, zero, zero, zero], axis=0),
            jnp.concatenate([none, hot, hot, zero, zero], axis=0),
            jnp.concatenate([none, zero, zero, hot, hot], axis=0),
        ]
        left = lhs_ref[first]
        looked = []
        for which in (0, 2):
            both = jnp.concatenate(rhs[which : which + 2], axis=1).astype(bf16)
            product = jnp.dot(left, both, preferred_element_type=f32)
            looked += [product[:, 0:LANES], product[:, LANES:]]
        return looked

    def scalars(looked, same, part):
        soft_sq, charge, six, twelve = looked
        root = lax.rsqrt(soft_sq)
        inverse = root * root
        inverse_two = inverse * inverse
        inverse_four = inverse_two * inverse_two
        dispersion = inverse_four * (twelve * (inverse_two * inverse) - six)
        coulomb = charge * (inverse * root - 2.0 * REACTION)
        switch = jnp.maximum((CUT_SQ + SOFT_CORE) - soft_sq, 0.0)
        scalar = (dispersion + coulomb) * (switch * switch)
        least = jnp.where(same, 1, -TILE_ATOMS)
        scalar = jnp.where(ahead >= least, scalar, 0.0)
        high = scalar.astype(bf16)
        scalar_ref[part, 0] = high
        scalar_ref[part, 1] = (scalar - high.astype(f32)).astype(bf16)

    def add_forces(first, place, part):
        left = row_block[first]
        right = col_block[place]
        left_x = jnp.concatenate([*split_three(left), jnp.zeros_like(left)], axis=0).astype(bf16)
        right_x = jnp.concatenate([*split_three(right), jnp.zeros_like(right)], axis=0).astype(bf16)
        high = scalar_ref[part, 0]
        low = scalar_ref[part, 1]
        sums_i = lax.dot_general(
            jnp.concatenate([right_x, right_x], axis=1),
            jnp.concatenate([high, low], axis=1),
            (((1,), (1,)), ((), ())),
            preferred_element_type=f32,
        )
        sums_j = jnp.dot(
            jnp.concatenate([left_x, left_x], axis=1),
            jnp.concatenate([high, low], axis=0),
            preferred_element_type=f32,
        )
        sums_i = sums_i[0:8] + sums_i[8:16] + sums_i[16:24]
        sums_j = sums_j[0:8] + sums_j[8:16] + sums_j[16:24]
        row_sum[first] += left * sums_i[6:7] - sums_i
        col_sum[place] += right * sums_j[6:7] - sums_j

    def find(slot):
        first = pairs_ref[0, slot]
        second = pairs_ref[1, slot]
        owner = second >> 2
        tile = second & 3
        same = (owner == my_row) & (first == my_col * tiles_dev + tile)
        far = ((owner >> 2) & 1) ^ my_zh
        place = ((owner & 24) << 2) | ((owner & 3) << 3) | (far << 2) | tile
        owner = first >> 2
        first = (((owner & 1) ^ my_core) << 5) | ((owner >> 1) << 2) | (first & 3)
        return first, place, same

    def step(index, before):
        found = [find(index * UNROLL + part) for part in range(UNROLL)]
        for start in range(0, UNROLL, LAG):
            looked = []
            for part in range(start, start + LAG):
                looked.append(features(*found[part][:2]))
                if part < LAG:
                    add_forces(before[2 * part], before[2 * part + 1], UNROLL - LAG + part)
                else:
                    add_forces(*found[part - LAG][:2], part - LAG)
            for part in range(start, start + LAG):
                scalars(looked[part - start], found[part][2], part)
        return tuple(place for first, second, _ in found[-LAG:] for place in (first, second))

    last = lax.fori_loop(
        0, pairs_ref[2, 0] // UNROLL, step, tuple(jnp.int32(0) for _ in range(2 * LAG))
    )
    for part in range(LAG):
        add_forces(last[2 * part], last[2 * part + 1], UNROLL - LAG + part)

    def gather_owners(index, carry):
        for source, start, target in (
            (row_sum, 0, own_force),
            (row_sum, half_tiles, other_force),
            *((col_sum, part * half_tiles, col_force.at[part]) for part in range(4)),
        ):
            for axis in range(3):
                target[index, axis] = source[
                    pl.ds(start + index * tiles_dev, tiles_dev), axis, :
                ]
        return carry

    lax.fori_loop(0, own_force.shape[0], gather_owners, 0, unroll=True)


def shards(positions, vel_half, charges, types, six_table, twelve_table, tile_pairs, pair_counts):
    atoms_dev = positions.shape[1]
    tiles_dev = TILES_DEV
    n_row = X_SIZE * ZH_SIZE * Y_SIZE
    n_col = N_COL
    n_xy = X_SIZE * Y_SIZE
    n_zl = n_col // CORES
    n_z = ZH_SIZE * n_zl
    my_zh = (lax.axis_index("row") >> 2) & 1
    my_zl = lax.axis_index("col") >> 1
    xy_groups = [
        [(x * ZH_SIZE + zh) * Y_SIZE + y for x in range(X_SIZE) for y in range(Y_SIZE)]
        for zh in range(ZH_SIZE)
    ]
    z_groups = [
        [
            ((x * ZH_SIZE + zh) * Y_SIZE + y) * n_col + zl * CORES + core
            for zh in range(ZH_SIZE)
            for zl in range(n_zl)
        ]
        for x in range(X_SIZE)
        for y in range(Y_SIZE)
        for core in range(CORES)
    ]
    core_swap = [(at, at ^ 1) for at in range(n_col)]

    smem = pl.BlockSpec(memory_space=pltpu.SMEM)
    vmem = pl.BlockSpec(memory_space=pltpu.VMEM)
    moved_pos, blocks = pl.pallas_call(
        pack_kernel,
        out_shape=(
            jax.ShapeDtypeStruct((3, atoms_dev), jnp.float32),
            jax.ShapeDtypeStruct((n_z, CHANNELS, tiles_dev, LANES), jnp.float32),
        ),
        in_specs=[vmem] * 4,
        out_specs=(vmem, vmem),
        name="pack_atoms",
    )(
        positions,
        vel_half,
        charges.reshape(tiles_dev, TILE_ATOMS),
        types.reshape(tiles_dev, TILE_ATOMS),
    )
    pad = ((0, TYPE_ROWS - BEAD_TYPES), (0, TYPE_ROWS - BEAD_TYPES))
    tables, pair_list = pl.pallas_call(
        table_kernel,
        out_shape=(
            jax.ShapeDtypeStruct((4 * TYPE_ROWS, TYPE_ROWS), jnp.bfloat16),
            jax.ShapeDtypeStruct((3, tile_pairs.shape[3]), jnp.int32),
        ),
        in_specs=[vmem] * 4,
        out_specs=(vmem, vmem),
        compiler_params=pltpu.CompilerParams(vmem_limit_bytes=4 * 2**20),
        name="tables",
    )(
        jnp.pad(six_table.T, pad),
        jnp.pad(twelve_table.T, pad),
        tile_pairs[0, 0],
        pair_counts,
    )
    z_blocks = lax.all_to_all(blocks, ("row", "col"), 0, 0, axis_index_groups=z_groups)
    z_blocks, tables, pair_list = lax.optimization_barrier((z_blocks, tables, pair_list))
    both, own_blocks = pl.pallas_call(
        join_kernel,
        out_shape=(
            jax.ShapeDtypeStruct((n_xy, ZH_SIZE, CHANNELS, tiles_dev, LANES), jnp.float32),
            jax.ShapeDtypeStruct((n_zl, CHANNELS, tiles_dev, LANES), jnp.float32),
        ),
        in_specs=[vmem],
        out_specs=(vmem, vmem),
        compiler_params=pltpu.CompilerParams(vmem_limit_bytes=4 * 2**20),
        name="join_halves",
    )(z_blocks)
    col_blocks = lax.all_to_all(both, "row", 0, 0, axis_index_groups=xy_groups)
    other_blocks = lax.ppermute(own_blocks, "col", core_swap)
    row_tiles = n_col * tiles_dev
    col_tiles = n_row * tiles_dev
    row_block, left_factors = pl.pallas_call(
        row_kernel,
        out_shape=(
            jax.ShapeDtypeStruct((row_tiles, 8, LANES), jnp.float32),
            jax.ShapeDtypeStruct((row_tiles, TILE_ATOMS, LANES), jnp.bfloat16),
        ),
        in_specs=[vmem, vmem, vmem],
        out_specs=(vmem, vmem),
        compiler_params=pltpu.CompilerParams(vmem_limit_bytes=16 * 2**20),
        cost_estimate=pl.CostEstimate(
            flops=2 * row_tiles * 96 * 128 * 128, bytes_accessed=4 * 2**20, transcendentals=0
        ),
        name="row_factors",
    )(own_blocks, other_blocks, tables)
    own_force, other_force, col_force = pl.pallas_call(
        pair_kernel,
        out_shape=(
            jax.ShapeDtypeStruct((n_zl, 3, tiles_dev, LANES), jnp.float32),
            jax.ShapeDtypeStruct((n_zl, 3, tiles_dev, LANES), jnp.float32),
            jax.ShapeDtypeStruct((n_row // n_zl, n_zl, 3, tiles_dev, LANES), jnp.float32),
        ),
        in_specs=[smem, vmem, vmem, vmem],
        out_specs=(vmem, vmem, vmem),
        scratch_shapes=[
            pltpu.VMEM((col_tiles, 8, LANES), jnp.float32),
            pltpu.VMEM((row_tiles, 8, LANES), jnp.float32),
            pltpu.VMEM((col_tiles, 8, LANES), jnp.float32),
            pltpu.VMEM((UNROLL, 2, TILE_ATOMS, LANES), jnp.bfloat16),
        ],
        compiler_params=pltpu.CompilerParams(vmem_limit_bytes=24 * 2**20),
        name="pair_forces",
    )(pair_list, row_block, left_factors, col_blocks.reshape(n_row, CHANNELS, tiles_dev, LANES))
    core_force = lax.ppermute(other_force, "col", core_swap)
    col_parts = lax.all_to_all(
        col_force.reshape(n_xy, ZH_SIZE, 3, tiles_dev, LANES),
        "row",
        0,
        0,
        axis_index_groups=xy_groups,
    )
    col_sum = jnp.sum(col_parts, axis=0)
    row_sum = own_force + core_force
    to_zh = lax.broadcasted_iota(jnp.int32, (ZH_SIZE, n_zl, 3, tiles_dev, LANES), 0)
    to_zl = lax.broadcasted_iota(jnp.int32, (ZH_SIZE, n_zl, 3, tiles_dev, LANES), 1)
    far_sum = jnp.where(to_zl == my_zl, col_sum[1][None, None], 0.0)
    z_parts = lax.all_to_all(
        jnp.where(to_zh == my_zh, row_sum[None], far_sum).reshape(n_z, 3, tiles_dev, LANES),
        ("row", "col"),
        0,
        0,
        axis_index_groups=z_groups,
    )
    force = jnp.sum(z_parts, axis=0) + col_sum[0]
    force_new = force.reshape(3, atoms_dev)
    velocity_new = vel_half + HALF_KICK * force_new
    return (moved_pos, force_new, velocity_new)


def solution(mesh):
    placed = (
        P(None, ("row", "col")),
        P(None, ("row", "col")),
        P(("row", "col")),
        P(("row", "col")),
        P(),
        P(),
        P("row", "col", None, None),
        P("row", "col"),
    )
    return jax.shard_map(
        shards,
        mesh=mesh,
        in_specs=placed,
        out_specs=(P(None, ("row", "col")), P(None, ("row", "col")), P(None, ("row", "col"))),
        check_vma=False,
    )
```

```python
import jax
import jax.numpy as jnp
from jax import lax
from jax.experimental import pallas as pl
from jax.experimental.pallas import tpu as pltpu
from jax.sharding import PartitionSpec as P

TILE_ATOMS = 128
TILES_DEV = 4
BEAD_TYPES = 18
LANES = 128

TIME_STEP = 0.02
HALF_KICK = 0.01 / 72.0
SOFT_CORE = 0.5
COULOMB = 9.262364
REACTION = 0.28935185
CUT_SQ = 1.44
CENTRE = 1.2

X_SIZE = 4
ZH_SIZE = 2
Y_SIZE = 4
N_COL = 16
CORES = 2
CHANNELS = 5
TYPE_ROWS = 24
UNROLL = 16
LAG = 4
PREPARED = 32

def split_three(values):
    upper = values.astype(jnp.bfloat16).astype(jnp.float32)
    rest = values - upper
    middle = rest.astype(jnp.bfloat16).astype(jnp.float32)
    return upper, middle, rest - middle


def pack_kernel(positions_ref, vel_ref, charge_ref, type_ref, moved_ref, blocks_ref):
    moved = positions_ref[...] + TIME_STEP * vel_ref[...]
    moved_ref[...] = moved
    centred = moved - CENTRE
    channels = [
        jnp.concatenate(
            [
                centred[axis : axis + 1, tile * TILE_ATOMS : (tile + 1) * TILE_ATOMS]
                for tile in range(TILES_DEV)
            ],
            axis=0,
        )
        for axis in range(3)
    ]
    channels += [charge_ref[...], type_ref[...].astype(jnp.float32)]
    for channel, values in enumerate(channels):
        for copy in range(blocks_ref.shape[0]):
            blocks_ref[copy, channel] = values


def join_kernel(z_ref, blocks_ref, own_ref):
    n_zl = own_ref.shape[0]
    my_zh = (lax.axis_index("row") // Y_SIZE) % ZH_SIZE
    my_zl = lax.axis_index("col") // CORES
    for half, zh in enumerate((my_zh, 1 - my_zh)):
        block = z_ref[zh * n_zl + my_zl]
        for copy in range(blocks_ref.shape[0]):
            blocks_ref[copy, half] = block
    for owner in range(n_zl):
        own_ref[owner] = z_ref[my_zh * n_zl + owner]


def table_kernel(six_ref, twelve_ref, pairs_ref, count_ref, table_ref, list_ref):
    parts = []
    for table, factor in ((six_ref, 6.0), (twelve_ref, 12.0)):
        scaled = table[...] * (factor / CUT_SQ**2)
        upper = scaled.astype(jnp.bfloat16).astype(jnp.float32)
        parts += [upper, scaled - upper]
    table_ref[...] = jnp.concatenate(parts, axis=0).astype(jnp.bfloat16)
    list_ref[0:2] = pairs_ref[...]
    list_ref[2:3] = jnp.broadcast_to(count_ref[...], (1, list_ref.shape[1]))


def hot_types(block):
    type_rows = lax.broadcasted_iota(jnp.int32, (TYPE_ROWS, LANES), 0).astype(jnp.float32)
    return (jnp.broadcast_to(block[5:6], (TYPE_ROWS, LANES)) == type_rows).astype(jnp.float32)


def spread(source, owner, target, start):
    x, y, z, charge, kind = [source[owner, channel] for channel in range(CHANNELS)]
    one = jnp.ones_like(x)
    channels = (x, y, z, x * x + y * y + z * z, charge, kind, one, jnp.zeros_like(x))
    for channel, values in enumerate(channels):
        target[pl.ds(start, TILES_DEV), channel, :] = values


def row_kernel(own_ref, other_ref, table_ref, row_block, lhs_ref):
    f32 = jnp.float32
    half_tiles = row_block.shape[0] // CORES
    sub8 = lax.broadcasted_iota(jnp.int32, (8, LANES), 0)
    scale = jnp.where(sub8 < 3, -2.0, jnp.where(sub8 == 4, COULOMB / CUT_SQ**2, 0.0)).astype(f32)

    def spread_owners(index, carry):
        spread(own_ref, index, row_block, index * TILES_DEV)
        spread(other_ref, index, row_block, half_tiles + index * TILES_DEV)
        return carry

    lax.fori_loop(0, own_ref.shape[0], spread_owners, 0, unroll=True)

    def prepare(index, carry):
        wholes = []
        for part in range(PREPARED):
            block = row_block[index * PREPARED + part]
            left = block * scale
            left = jnp.where(sub8 == 3, 1.0, left)
            left = jnp.where(sub8 == 6, block[3:4] + SOFT_CORE, left)
            upper, middle, _ = split_three(left)
            coefs = jnp.dot(
                table_ref[...],
                hot_types(block).astype(jnp.bfloat16),
                preferred_element_type=f32,
            )
            wholes.append(jnp.concatenate([upper, upper, middle, middle, coefs], axis=0))
        for part in range(PREPARED):
            lhs_ref[index * PREPARED + part] = wholes[part].T.astype(jnp.bfloat16)
        return carry

    lax.fori_loop(0, row_block.shape[0] // PREPARED, prepare, 0)


def pair_kernel(
    pairs_ref, row_block, lhs_ref, col_ref,
    own_force, other_force, col_force,
    col_block, row_sum, col_sum, scalar_ref
):
    tiles_dev = TILES_DEV
    my_row = lax.axis_index("row")
    my_col = lax.axis_index("col")
    my_zh = (my_row // Y_SIZE) % ZH_SIZE
    my_core = my_col % CORES
    half_tiles = row_block.shape[0] // CORES
    f32 = jnp.float32
    bf16 = jnp.bfloat16
    sub8 = lax.broadcasted_iota(jnp.int32, (8, LANES), 0)
    sub8 = lax.broadcasted_iota(jnp.int32, (8, LANES), 0)
    shape = (TILE_ATOMS, LANES)
    ahead = lax.broadcasted_iota(jnp.int32, shape, 1) - lax.broadcasted_iota(jnp.int32, shape, 0)

    row_sum[...] = jnp.zeros(row_sum.shape, f32)
    col_sum[...] = jnp.zeros(col_sum.shape, f32)
    scalar_ref[UNROLL - LAG :] = jnp.zeros((LAG, *scalar_ref.shape[1:]), bf16)

    def spread_owners(index, carry):
        for part in range(4):
            owner = index * 4 + part
            spread(col_ref, owner, col_block, owner * TILES_DEV)
        return carry

    lax.fori_loop(0, col_ref.shape[0] // 4, spread_owners, 0)

    def features(first, place):
        right = col_block[place]
        upper, middle, _ = split_three(right)
        hot = hot_types(right)
        zero = jnp.zeros_like(hot)
        dist = [jnp.where(sub8 == 4, 0.0, part) for part in (upper, middle)]
        charge = [jnp.where(sub8 == 4, part, 0.0) for part in (upper, middle)]
        none = jnp.zeros((32, LANES), f32)
        rhs = [
            jnp.concatenate([*dist, *dist, zero, zero, zero, zero], axis=0),
            jnp.concatenate([*charge, *charge, zero, zero, zero, zero], axis=0),
            jnp.concatenate([none, hot, hot, zero, zero], axis=0),
            jnp.concatenate([none, zero, zero, hot, hot], axis=0),
        ]
        left = lhs_ref[first]
        looked = []
        for which in (0, 2):
            both = jnp.concatenate(rhs[which : which + 2], axis=1).astype(bf16)
            product = jnp.dot(left, both, preferred_element_type=f32)
            looked += [product[:, 0:LANES], product[:, LANES:]]
        return looked

    def scalars(looked, same, part):
        soft_sq, charge, six, twelve = looked
        root = lax.rsqrt(soft_sq)
        inverse = root * root
        inverse_two = inverse * inverse
        inverse_four = inverse_two * inverse_two
        dispersion = inverse_four * (twelve * (inverse_two * inverse) - six)
        coulomb = charge * (inverse * root - 2.0 * REACTION)
        switch = jnp.maximum((CUT_SQ + SOFT_CORE) - soft_sq, 0.0)
        scalar = (dispersion + coulomb) * (switch * switch)
        least = jnp.where(same, 1, -TILE_ATOMS)
        scalar = jnp.where(ahead >= least, scalar, 0.0)
        high = scalar.astype(bf16)
        scalar_ref[part, 0] = high
        scalar_ref[part, 1] = (scalar - high.astype(f32)).astype(bf16)

    def add_forces(first, place, part):
        left = row_block[first]
        right = col_block[place]
        left_x = jnp.concatenate([*split_three(left), jnp.zeros_like(left)], axis=0).astype(bf16)
        right_x = jnp.concatenate([*split_three(right), jnp.zeros_like(right)], axis=0).astype(bf16)
        high = scalar_ref[part, 0]
        low = scalar_ref[part, 1]
        sums_i = lax.dot_general(
            jnp.concatenate([right_x, right_x], axis=1),
            jnp.concatenate([high, low], axis=1),
            (((1,), (1,)), ((), ())),
            preferred_element_type=f32,
        )
        sums_j = jnp.dot(
            jnp.concatenate([left_x, left_x], axis=1),
            jnp.concatenate([high, low], axis=0),
            preferred_element_type=f32,
        )
        sums_i = sums_i[0:8] + sums_i[8:16] + sums_i[16:24]
        sums_j = sums_j[0:8] + sums_j[8:16] + sums_j[16:24]
        row_sum[first] += left * sums_i[6:7] - sums_i
        col_sum[place] += right * sums_j[6:7] - sums_j

    def find(slot):
        first = pairs_ref[0, slot]
        second = pairs_ref[1, slot]
        owner = second >> 2
        tile = second & 3
        same = (owner == my_row) & (first == my_col * tiles_dev + tile)
        far = ((owner >> 2) & 1) ^ my_zh
        place = ((owner & 24) << 2) | ((owner & 3) << 3) | (far << 2) | tile
        owner = first >> 2
        first = (((owner & 1) ^ my_core) << 5) | ((owner >> 1) << 2) | (first & 3)
        return first, place, same

    def step(index, before):
        found = [find(index * UNROLL + part) for part in range(UNROLL)]
        for start in range(0, UNROLL, LAG):
            looked = []
            for part in range(start, start + LAG):
                looked.append(features(*found[part][:2]))
                if part < LAG:
                    add_forces(before[2 * part], before[2 * part + 1], UNROLL - LAG + part)
                else:
                    add_forces(*found[part - LAG][:2], part - LAG)
            for part in range(start, start + LAG):
                scalars(looked[part - start], found[part][2], part)
        return tuple(place for first, second, _ in found[-LAG:] for place in (first, second))

    last = lax.fori_loop(
        0, pairs_ref[2, 0] // UNROLL, step, tuple(jnp.int32(0) for _ in range(2 * LAG))
    )
    for part in range(LAG):
        add_forces(last[2 * part], last[2 * part + 1], UNROLL - LAG + part)

    def gather_owners(index, carry):
        for source, start, target in (
            (row_sum, 0, own_force),
            (row_sum, half_tiles, other_force),
            *((col_sum, part * half_tiles, col_force.at[part]) for part in range(4)),
        ):
            for axis in range(3):
                target[index, axis] = source[
                    pl.ds(start + index * tiles_dev, tiles_dev), axis, :
                ]
        return carry

    lax.fori_loop(0, own_force.shape[0], gather_owners, 0, unroll=True)


def shards(positions, vel_half, charges, types, six_table, twelve_table, tile_pairs, pair_counts):
    atoms_dev = positions.shape[1]
    tiles_dev = TILES_DEV
    n_row = X_SIZE * ZH_SIZE * Y_SIZE
    n_col = N_COL
    n_xy = X_SIZE * Y_SIZE
    n_zl = n_col // CORES
    n_z = ZH_SIZE * n_zl
    my_zh = (lax.axis_index("row") >> 2) & 1
    my_zl = lax.axis_index("col") >> 1
    xy_groups = [
        [(x * ZH_SIZE + zh) * Y_SIZE + y for x in range(X_SIZE) for y in range(Y_SIZE)]
        for zh in range(ZH_SIZE)
    ]
    z_groups = [
        [
            ((x * ZH_SIZE + zh) * Y_SIZE + y) * n_col + zl * CORES + core
            for zh in range(ZH_SIZE)
            for zl in range(n_zl)
        ]
        for x in range(X_SIZE)
        for y in range(Y_SIZE)
        for core in range(CORES)
    ]
    core_swap = [(at, at ^ 1) for at in range(n_col)]

    smem = pl.BlockSpec(memory_space=pltpu.SMEM)
    vmem = pl.BlockSpec(memory_space=pltpu.VMEM)
    moved_pos, blocks = pl.pallas_call(
        pack_kernel,
        out_shape=(
            jax.ShapeDtypeStruct((3, atoms_dev), jnp.float32),
            jax.ShapeDtypeStruct((n_z, CHANNELS, tiles_dev, LANES), jnp.float32),
        ),
        in_specs=[vmem] * 4,
        out_specs=(vmem, vmem),
        name="pack_atoms",
    )(
        positions,
        vel_half,
        charges.reshape(tiles_dev, TILE_ATOMS),
        types.reshape(tiles_dev, TILE_ATOMS),
    )
    pad = ((0, TYPE_ROWS - BEAD_TYPES), (0, TYPE_ROWS - BEAD_TYPES))
    tables, pair_list = pl.pallas_call(
        table_kernel,
        out_shape=(
            jax.ShapeDtypeStruct((4 * TYPE_ROWS, TYPE_ROWS), jnp.bfloat16),
            jax.ShapeDtypeStruct((3, tile_pairs.shape[3]), jnp.int32),
        ),
        in_specs=[vmem] * 4,
        out_specs=(vmem, vmem),
        compiler_params=pltpu.CompilerParams(vmem_limit_bytes=4 * 2**20),
        name="tables",
    )(
        jnp.pad(six_table.T, pad),
        jnp.pad(twelve_table.T, pad),
        tile_pairs[0, 0],
        pair_counts,
    )
    z_blocks = lax.all_to_all(blocks, ("row", "col"), 0, 0, axis_index_groups=z_groups)
    z_blocks, tables, pair_list = lax.optimization_barrier((z_blocks, tables, pair_list))
    both, own_blocks = pl.pallas_call(
        join_kernel,
        out_shape=(
            jax.ShapeDtypeStruct((n_xy, ZH_SIZE, CHANNELS, tiles_dev, LANES), jnp.float32),
            jax.ShapeDtypeStruct((n_zl, CHANNELS, tiles_dev, LANES), jnp.float32),
        ),
        in_specs=[vmem],
        out_specs=(vmem, vmem),
        compiler_params=pltpu.CompilerParams(vmem_limit_bytes=4 * 2**20),
        name="join_halves",
    )(z_blocks)
    col_blocks = lax.all_to_all(both, "row", 0, 0, axis_index_groups=xy_groups)
    other_blocks = lax.ppermute(own_blocks, "col", core_swap)
    row_tiles = n_col * tiles_dev
    col_tiles = n_row * tiles_dev
    row_block, left_factors = pl.pallas_call(
        row_kernel,
        out_shape=(
            jax.ShapeDtypeStruct((row_tiles, 8, LANES), jnp.float32),
            jax.ShapeDtypeStruct((row_tiles, TILE_ATOMS, LANES), jnp.bfloat16),
        ),
        in_specs=[vmem, vmem, vmem],
        out_specs=(vmem, vmem),
        compiler_params=pltpu.CompilerParams(vmem_limit_bytes=16 * 2**20),
        cost_estimate=pl.CostEstimate(
            flops=2 * row_tiles * 96 * 128 * 128, bytes_accessed=4 * 2**20, transcendentals=0
        ),
        name="row_factors",
    )(own_blocks, other_blocks, tables)
    own_force, other_force, col_force = pl.pallas_call(
        pair_kernel,
        out_shape=(
            jax.ShapeDtypeStruct((n_zl, 3, tiles_dev, LANES), jnp.float32),
            jax.ShapeDtypeStruct((n_zl, 3, tiles_dev, LANES), jnp.float32),
            jax.ShapeDtypeStruct((n_row // n_zl, n_zl, 3, tiles_dev, LANES), jnp.float32),
        ),
        in_specs=[smem, vmem, vmem, vmem],
        out_specs=(vmem, vmem, vmem),
        scratch_shapes=[
            pltpu.VMEM((col_tiles, 8, LANES), jnp.float32),
            pltpu.VMEM((row_tiles, 8, LANES), jnp.float32),
            pltpu.VMEM((col_tiles, 8, LANES), jnp.float32),
            pltpu.VMEM((UNROLL, 2, TILE_ATOMS, LANES), jnp.bfloat16),
        ],
        compiler_params=pltpu.CompilerParams(vmem_limit_bytes=24 * 2**20),
        name="pair_forces",
    )(pair_list, row_block, left_factors, col_blocks.reshape(n_row, CHANNELS, tiles_dev, LANES))
    core_force = lax.ppermute(other_force, "col", core_swap)
    col_parts = lax.all_to_all(
        col_force.reshape(n_xy, ZH_SIZE, 3, tiles_dev, LANES),
        "row",
        0,
        0,
        axis_index_groups=xy_groups,
    )
    col_sum = jnp.sum(col_parts, axis=0)
    row_sum = own_force + core_force
    to_zh = lax.broadcasted_iota(jnp.int32, (ZH_SIZE, n_zl, 3, tiles_dev, LANES), 0)
    to_zl = lax.broadcasted_iota(jnp.int32, (ZH_SIZE, n_zl, 3, tiles_dev, LANES), 1)
    far_sum = jnp.where(to_zl == my_zl, col_sum[1][None, None], 0.0)
    z_parts = lax.all_to_all(
        jnp.where(to_zh == my_zh, row_sum[None], far_sum).reshape(n_z, 3, tiles_dev, LANES),
        ("row", "col"),
        0,
        0,
        axis_index_groups=z_groups,
    )
    force = jnp.sum(z_parts, axis=0) + col_sum[0]
    force_new = force.reshape(3, atoms_dev)
    velocity_new = vel_half + HALF_KICK * force_new
    return (moved_pos, force_new, velocity_new)


def solution(mesh):
    placed = (
        P(None, ("row", "col")),
        P(None, ("row", "col")),
        P(("row", "col")),
        P(("row", "col")),
        P(),
        P(),
        P("row", "col", None, None),
        P("row", "col"),
    )
    return jax.shard_map(
        shards,
        mesh=mesh,
        in_specs=placed,
        out_specs=(P(None, ("row", "col")), P(None, ("row", "col")), P(None, ("row", "col"))),
        check_vma=False,
    )
```
